256 devices in a mesh: inst: 64 (over x_lo, z, y), tp: 4 (over x_hi, core).
Axes of the slice: x: 4 (x_hi: 2, x_lo: 2; x = x_hi * 2 + x_lo), y: 4, z: 8, core: 2. Of those that a mesh axis runs over, the one named last changes fastest.
Arguments:
- res_keys: bfloat16 [384, 4, 1024, 128], P('inst', 'tp'), may hold values from -12 to 12, as said below
- res_values: bfloat16 [384, 4, 1024, 128], P('inst', 'tp'), may hold values from -6 to 6
- pool_keys: bfloat16 [1024, 4, 128, 128], P('inst', 'tp'), may hold values from -12 to 12
- pool_values: bfloat16 [1024, 4, 128, 128], P('inst', 'tp'), may hold values from -6 to 6
- queries: bfloat16 [640, 32, 4, 128], P('inst', 'tp'), may hold values from -25 to 25
- new_keys: bfloat16 [640, 4, 4, 128], P('inst', 'tp'), may hold values from -6 to 6
- new_values: bfloat16 [640, 4, 4, 128], P('inst', 'tp'), may hold values from -6 to 6
- res_len: int32 [384], replicated, may hold values from 1 to 1024, as said below
- new_len: int32 [256], replicated, may hold values from 1921 to 2048, as said below
- page_source: int32 [64, 64], replicated, may hold values from 0 to 63, as said below
- page_index: int32 [64, 64], replicated, may hold values from 0 to 15
- partner_bit: int32 [64], replicated, may hold values from 0 to 1, as said below
- migrate_out: int32 [64], replicated, may hold values from 1 to 2
- out_weight: bfloat16 [4096, 4096], P('tp'), may hold values from -0.09375 to 0.09375
Outputs:
- mixed: bfloat16 [3072, 4096], P('inst', 'tp')
The draws below stay inside these ranges and needn't reach their ends.
Inputs may be any that keep to these rules, and one draw needn't show every extreme that they name: `res_keys`: scores of the cache reach far beyond one in some rows. `res_len`: 1024 is reached by some request. `new_len`: 2048 is reached by some request; every page of a new request is live. `page_source`: each destination takes at most 2 pages from one source, and exactly 2 from some source. `partner_bit`: below 2, the same for all instances of an aligned group of 2 ** 2, so the pairs form a perfect matching inside each group.
All inputs are finite; a program needn't handle non-finite values.
Results may differ from the reference program's by a relative error of at most 0.008.
Values may be sent and summed in bfloat16 or wider, within the bound.
A program may use at most 128 MiB of HBM per device.

```python
import math
import jax
import jax.numpy as jnp
from jax import lax

D = 4096
QHEADS = 32
KVHEADS = 4
HD = 128
PAGE = 128
STEPS = 4
RES = 6
CTX = 1024
MIG = 2
NEW = 4
NPAGES = 16
POOL = 16
MATCH_BITS = 2
INSTANCES = 64
IN_PAGES = 64
CAP = 2
REQS = 10
SLOTS = 12


def draw_partner_bit(key, part):
    key = jax.random.fold_in(key, 3)
    group_count = INSTANCES // 2 ** MATCH_BITS
    group_bits = jax.random.randint(key, (group_count,), 0, MATCH_BITS)
    instance = jnp.arange(INSTANCES, dtype=jnp.int32)
    return group_bits[instance // 2 ** MATCH_BITS].astype(jnp.int32)


def draw_res_keys(key, part):
    key = jax.random.fold_in(key, 11)
    full_shape = (INSTANCES * RES, KVHEADS, CTX, HD)
    base_draw = jnp.clip(jax.random.normal(key, full_shape, jnp.float32), -6.0, 6.0)
    return base_draw.astype(jnp.bfloat16)


def draw_pool_keys(key, part):
    key = jax.random.fold_in(key, 13)
    full_shape = (INSTANCES * POOL, KVHEADS, PAGE, HD)
    base_draw = jnp.clip(jax.random.normal(key, full_shape, jnp.float32), -6.0, 6.0)
    return base_draw.astype(jnp.bfloat16)


def draw_queries(key, part):
    key = jax.random.fold_in(key, 17)
    full_shape = (INSTANCES * (RES + NEW), QHEADS, STEPS, HD)
    base_draw = jnp.clip(jax.random.normal(key, full_shape, jnp.float32), -6.0, 6.0)
    return base_draw.astype(jnp.bfloat16)


def draw_res_len(key, part):
    key = jax.random.fold_in(key, 7)
    lengths = jax.random.randint(key, (INSTANCES * RES,), max(1, CTX // 8), CTX + 1)
    top_slot = jax.random.randint(jax.random.fold_in(key, 1), (), 0, INSTANCES * RES)
    return lengths.at[top_slot].set(CTX).astype(jnp.int32)


def draw_new_len(key, part):
    key = jax.random.fold_in(key, 9)
    lengths = jax.random.randint(key, (INSTANCES * NEW,), (NPAGES - 1) * PAGE + 1, NPAGES * PAGE + 1)
    top_slot = jax.random.randint(jax.random.fold_in(key, 1), (), 0, INSTANCES * NEW)
    return lengths.at[top_slot].set(NPAGES * PAGE).astype(jnp.int32)


def draw_page_source(key, part):
    key = jax.random.fold_in(key, 5)
    candidates = INSTANCES * CAP

    def one_destination(destination, dest_key):
        priority = jax.random.permutation(dest_key, candidates).astype(jnp.int32)
        source_of = jnp.arange(candidates, dtype=jnp.int32) // CAP
        forced = source_of == (destination + 1) % INSTANCES
        priority = jnp.where(forced, -1, priority)
        picked = jnp.argsort(priority, stable=True)[:IN_PAGES]
        chosen_sources = source_of[picked]
        shuffle = jax.random.permutation(jax.random.fold_in(dest_key, 1), IN_PAGES)
        return chosen_sources[shuffle]
    dest_keys = jax.random.split(key, INSTANCES)
    return jax.vmap(one_destination)(jnp.arange(INSTANCES, dtype=jnp.int32), dest_keys).astype(jnp.int32)


def place_ends(entries, stream_key, smallest, high):
    shape = entries.shape
    spot = [jax.random.randint(jax.random.fold_in(stream_key, axis), (), 0, shape[axis]) for axis in range(len(shape))]
    entries = entries.at[tuple(spot)].set(smallest)
    longest = shape.index(max(shape))
    spot[longest] = (spot[longest] + 1) % shape[longest]
    return entries.at[tuple(spot)].set(high)


def steps_of(stream_key, extent, pieces, low, high):
    loudness, own = 1.0, jax.random.fold_in(stream_key, 6)
    for axis_at, shards_of in pieces:
        steps = jnp.exp(jax.random.uniform(jax.random.fold_in(own, axis_at), (shards_of,), jnp.float32, low / len(pieces), high / len(pieces)))
        loudness = loudness * jnp.repeat(steps, extent[axis_at] // shards_of).reshape([-1 if axis == axis_at else 1 for axis in range(len(extent))])
    return loudness


def bell_draw(rng, dims, scale, most, pieces=(), kind=jnp.bfloat16):
    drawn = jax.random.normal(rng, dims, jnp.float32) * scale
    if len(pieces) > 0:
        drawn = steps_of(rng, dims, pieces, -0.22, 0.18) * drawn
    return jnp.clip(drawn, min=-most, max=most).astype(kind)


def setup_inputs(seed: int = 0) -> dict:
    streams_of = jax.random.split(jax.random.key(seed), 15)
    res_keys = draw_res_keys(jax.random.fold_in(streams_of[14], 71), 0)
    res_values = bell_draw(streams_of[1], (INSTANCES * RES, KVHEADS, CTX, HD), 1.0, 6.0, ((0, 64), (1, 4)))
    pool_keys = draw_pool_keys(jax.random.fold_in(streams_of[14], 71), 0)
    pool_values = bell_draw(streams_of[3], (INSTANCES * POOL, KVHEADS, PAGE, HD), 1.0, 6.0, ((0, 64), (1, 4)))
    queries = draw_queries(jax.random.fold_in(streams_of[14], 71), 0)
    new_keys = bell_draw(streams_of[5], (INSTANCES * REQS, KVHEADS, STEPS, HD), 1.0, 6.0, ((0, 64), (1, 4)))
    new_values = bell_draw(streams_of[6], (INSTANCES * REQS, KVHEADS, STEPS, HD), 1.0, 6.0, ((0, 64), (1, 4)))
    res_len = draw_res_len(jax.random.fold_in(streams_of[14], 71), 0)
    new_len = draw_new_len(jax.random.fold_in(streams_of[14], 71), 0)
    page_source = draw_page_source(jax.random.fold_in(streams_of[14], 71), 0)
    page_index = place_ends(jax.random.randint(streams_of[10], (INSTANCES, IN_PAGES), 0, POOL), jax.random.fold_in(streams_of[10], 1), 0, POOL - 1).astype(jnp.int32)
    partner_bit = draw_partner_bit(jax.random.fold_in(streams_of[14], 71), 0)
    migrate_out = place_ends(jax.random.randint(streams_of[12], (INSTANCES,), 1, MIG + 1), jax.random.fold_in(streams_of[12], 1), 1, MIG).astype(jnp.int32)
    out_weight = bell_draw(streams_of[13], (QHEADS * HD, D), (QHEADS * HD) ** -0.5, 0.09375, ((0, 4),))
    return {"res_keys": res_keys, "res_values": res_values, "pool_keys": pool_keys, "pool_values": pool_values, "queries": queries, "new_keys": new_keys, "new_values": new_values, "res_len": res_len, "new_len": new_len, "page_source": page_source, "page_index": page_index, "partner_bit": partner_bit, "migrate_out": migrate_out, "out_weight": out_weight}


def attend(cache_keys, values, length, queries, fresh_keys, fresh_values):
    heads_kv, context, head_dim = cache_keys.shape
    group_size = queries.shape[0] // heads_kv
    step_count = queries.shape[1]
    score_scale = 1.0 / math.sqrt(head_dim)
    grouped = queries.reshape(heads_kv, group_size, step_count, head_dim).astype(jnp.float32)
    old_scores = jnp.einsum('kgtd,kcd->kgtc', grouped, cache_keys.astype(jnp.float32)) * score_scale
    new_scores = jnp.einsum('kgtd,ksd->kgts', grouped, fresh_keys.astype(jnp.float32)) * score_scale
    old_live = (jnp.arange(context, dtype=jnp.int32) < length)[None, None, None, :]
    positions = jnp.arange(step_count, dtype=jnp.int32)
    new_live = (positions[None, :] <= positions[:, None])[None, None]
    old_scores = jnp.where(old_live, old_scores, -jnp.inf)
    new_scores = jnp.where(new_live, new_scores, -jnp.inf)
    peak_score = jnp.maximum(lax.optimization_barrier(jnp.max(old_scores, axis=-1)), lax.optimization_barrier(jnp.max(new_scores, axis=-1)))[..., None]
    old_exp = jnp.exp(old_scores - peak_score)
    new_exp = jnp.exp(new_scores - peak_score)
    weight_total = lax.optimization_barrier(jnp.sum(old_exp, axis=-1, keepdims=True)) + lax.optimization_barrier(jnp.sum(new_exp, axis=-1, keepdims=True))
    old_weight = (old_exp / weight_total).astype(jnp.bfloat16)
    new_weight = (new_exp / weight_total).astype(jnp.bfloat16)
    attended = jnp.einsum('kgtc,kcd->kgtd', old_weight.astype(jnp.float32), values.astype(jnp.float32))
    attended = attended + jnp.einsum('kgts,ksd->kgtd', new_weight.astype(jnp.float32), fresh_values.astype(jnp.float32))
    return attended.reshape(heads_kv * group_size, step_count, head_dim).astype(jnp.bfloat16)

def reference(res_keys, res_values, pool_keys, pool_values, queries, new_keys, new_values, res_len, new_len, page_source, page_index, partner_bit, migrate_out, out_weight):
    req_count = RES + NEW

    def per_instance(instance):
        own_start = instance * RES
        own_keys = lax.dynamic_slice_in_dim(res_keys, own_start, RES, 0)
        own_values = lax.dynamic_slice_in_dim(res_values, own_start, RES, 0)
        own_len = lax.dynamic_slice_in_dim(res_len, own_start, RES, 0)
        inst_queries = lax.dynamic_slice_in_dim(queries, instance * req_count, req_count, 0)
        inst_new_keys = lax.dynamic_slice_in_dim(new_keys, instance * req_count, req_count, 0)
        inst_new_values = lax.dynamic_slice_in_dim(new_values, instance * req_count, req_count, 0)
        own_out = jax.vmap(attend)(own_keys, own_values, own_len, inst_queries[:RES], inst_new_keys[:RES], inst_new_values[:RES])
        hand_here = migrate_out[instance]
        keep_mask = jnp.arange(RES, dtype=jnp.int32) < RES - hand_here
        own_out = jnp.where(keep_mask[:, None, None, None], own_out, jnp.zeros_like(own_out))
        partner = jnp.bitwise_xor(instance, jnp.left_shift(jnp.int32(1), partner_bit[instance]))
        hand_there = migrate_out[partner]
        guest_start = partner * RES + RES - MIG
        guest_row = partner * req_count + RES - MIG
        guest_out = jax.vmap(attend)(lax.dynamic_slice_in_dim(res_keys, guest_start, MIG, 0), lax.dynamic_slice_in_dim(res_values, guest_start, MIG, 0), lax.dynamic_slice_in_dim(res_len, guest_start, MIG, 0), lax.dynamic_slice_in_dim(queries, guest_row, MIG, 0), lax.dynamic_slice_in_dim(new_keys, guest_row, MIG, 0), lax.dynamic_slice_in_dim(new_values, guest_row, MIG, 0))
        guest_mask = jnp.arange(MIG, dtype=jnp.int32) >= MIG - hand_there
        guest_out = jnp.where(guest_mask[:, None, None, None], guest_out, jnp.zeros_like(guest_out))
        pool_rows = (page_source[instance] * POOL + page_index[instance]).astype(jnp.int32)

        def arrange(page_block):
            picked = page_block[pool_rows]
            picked = picked.reshape(NEW, NPAGES, KVHEADS, PAGE, HD).transpose(0, 2, 1, 3, 4)
            return picked.reshape(NEW, KVHEADS, NPAGES * PAGE, HD)
        new_lengths = lax.dynamic_slice_in_dim(new_len, instance * NEW, NEW, 0)
        new_out = jax.vmap(attend)(arrange(pool_keys), arrange(pool_values), new_lengths, inst_queries[RES:], inst_new_keys[RES:], inst_new_values[RES:])
        all_slots = jnp.concatenate([own_out, guest_out, new_out], axis=0)
        flat_rows = all_slots.transpose(0, 2, 1, 3).reshape(SLOTS * STEPS, QHEADS * HD)
        return jnp.dot(flat_rows, out_weight, preferred_element_type=jnp.float32).astype(jnp.bfloat16)
    mixed = lax.map(per_instance, jnp.arange(INSTANCES, dtype=jnp.int32))
    return mixed.reshape(INSTANCES * SLOTS * STEPS, D)
```

```python
import math

import jax
import jax.numpy as jnp
from jax import lax
from jax.experimental import pallas as pl
from jax.experimental.pallas import tpu as pltpu
from jax.sharding import PartitionSpec as P

MESH = pl.DeviceIdType.MESH
NX, NZ, NY = 2, 8, 4
PEERS = NX * NY
TP = 4
RES, NEW, MIG = 6, 4, 2
STEPS = 4
ROWS = 32
HD = 128
PAGE = 128
NPAGES = 16
LOW = -1e30
GROUPS = 12
NT = (((1,), (1,)), ((), ()))
NN = (((1,), (0,)), ((), ()))


def mirror(r):
    dx, dy = divmod(r, NY)
    return dx * NY + (NY - dy) % NY


def iota(shape, axis):
    return lax.broadcasted_iota(jnp.int32, shape, axis)


def dot(a, b, dims=NN):
    return lax.dot_general(a, b, dims, preferred_element_type=jnp.float32)


def kernel(
    res_len,
    new_len,
    partner_bit,
    migrate_out,
    page_source,
    page_index,
    queries,
    new_keys,
    new_values,
    res_keys,
    res_values,
    pool_keys,
    pool_values,
    weight,
    out,
    rk,
    rv,
    pk,
    pv,
    wv,
    tab_v,
    tab,
    q1,
    fw,
    q2,
    r1s,
    r1,
    sts,
    st,
    r2s,
    ls,
    fin,
    lf,
    att,
    guest,
    attm,
    xres,
    xnew,
    own1,
    own2,
    rs1s,
    rs1,
    rs2s,
    rs2,
    load_sem,
    q1_send,
    q1_recv,
    q2_send,
    q2_recv,
    r1_send,
    r1_recv,
    st_send,
    st_recv,
    r2_send,
    r2_recv,
    lf_send,
    lf_recv,
    mig_send,
    mig_recv,
    rs1_send,
    rs1_recv,
    rs2_send,
    rs2_recv,
):
    me = lax.axis_index("inst")
    tp = lax.axis_index("tp")
    y = lax.rem(me, NY)
    z = lax.rem(lax.div(me, NY), NZ)
    x = lax.div(me, NY * NZ)
    hi = lax.div(tp, 2)
    core = lax.rem(tp, 2)
    scale = 1.0 / math.sqrt(HD)

    def inst_at(xx, zz, yy):
        return (xx * NZ + zz) * NY + yy

    def plane(r, zz):
        dx, dy = divmod(r, NY)
        return inst_at(lax.rem(x + dx, NX), zz, lax.rem(y + dy, NY))

    def line(zi):
        return inst_at(x, lax.rem(z + zi, NZ), y)

    def tp_peer(o):
        return lax.rem(hi + o // 2, 2) * 2 + lax.rem(core + o % 2, 2)

    def order(i):
        odd = lax.rem(i, 2)
        return lax.rem(odd * lax.div(i + 1, 2) + (1 - odd) * (NZ - lax.div(i, 2)), NZ)

    def remote(src, dst, send, recv, inst, t=tp):
        return pltpu.make_async_remote_copy(
            src_ref=src,
            dst_ref=dst,
            send_sem=send,
            recv_sem=recv,
            device_id=(inst, t),
            device_id_type=MESH,
        )

    def drain(ref, sem):
        pltpu.make_async_copy(ref, ref, sem).wait()

    loads = [
        pltpu.make_async_copy(src, dst, load_sem.at[k])
        for k, (src, dst) in enumerate(
            [
                (res_keys, rk),
                (res_values, rv),
                (pool_keys, pk),
                (pool_values, pv),
                (weight, wv),
            ]
        )
    ]
    for copy in loads:
        copy.start()

    barrier = pltpu.get_barrier_semaphore()
    for zi in range(1, NZ):
        pl.semaphore_signal(barrier, inc=1, device_id=(line(zi), tp), device_id_type=MESH)
    for r in range(1, PEERS):
        pl.semaphore_signal(barrier, inc=1, device_id=(plane(r, z), tp), device_id_type=MESH)
    for o in range(1, TP):
        pl.semaphore_signal(barrier, inc=1, device_id=(me, tp_peer(o)), device_id_type=MESH)
    pl.semaphore_wait(barrier, NZ - 1 + PEERS - 1 + TP - 1)

    seq = [0, 1, 7, 2, 6, 3, 5, 4]
    q1_copies = []
    for i in range(1, NZ):
        zi = seq[i]
        back = seq.index(NZ - zi)
        copy = remote(
            queries.at[pl.ds(RES * ROWS, NEW * ROWS)],
            q1.at[back],
            q1_send.at[i],
            q1_recv.at[back],
            line(zi),
        )
        copy.start()
        q1_copies.append(copy)
    q1[0] = queries[RES * ROWS :, :]

    places = page_source.shape[1]
    count = page_source.shape[0]
    source = page_source[...]
    slot = page_index[...]
    place = iota((count, places), 1)
    lane = iota((count, HD), 1)
    table = jnp.zeros((count, HD), jnp.int32)
    for r in range(PEERS):
        hit = source == plane(r, z)
        first = jnp.min(jnp.where(hit, place, places), axis=1, keepdims=True)
        last = jnp.max(jnp.where(hit, place, -1), axis=1, keepdims=True)
        last = jnp.where(last > first, last, places)
        table = jnp.where(lane == 2 * r, first, table)
        table = jnp.where(lane == 2 * r + 1, last, table)
        if r == 0:
            for c, p in ((0, first), (1, last)):
                page = jnp.max(jnp.where(place == p, slot, 0), axis=1, keepdims=True)
                table = jnp.where(lane == 2 * PEERS + c, page, table)
    tab_v[...] = table
    tab_copy = pltpu.make_async_copy(tab_v, tab, load_sem.at[5])
    tab_copy.start()
    tab_copy.wait()

    def forward(i):
        dest = line(order(i))
        block = [q1[i, pl.ds(n * ROWS, ROWS), :] for n in range(NEW)]
        for r in range(PEERS):
            for c in range(2):
                n = lax.div(tab[dest, 2 * r + c], NPAGES)
                q = lax.select(
                    n == 0,
                    block[0],
                    lax.select(n == 1, block[1], lax.select(n == 2, block[2], block[3])),
                )
                if r == 0:
                    q2[i, 0, pl.ds(c * ROWS, ROWS), :] = q
                else:
                    fw[i, r, pl.ds(c * ROWS, ROWS), :] = q
            if r > 0:
                remote(
                    fw.at[i, r], q2.at[i, mirror(r)], q2_send.at[i], q2_recv.at[i], plane(r, z)
                ).start()

    forward(jnp.int32(0))

    def forward_step(i, carry):
        drain(q1.at[i], q1_recv.at[i])
        forward(i)
        return carry

    lax.fori_loop(1, NZ, forward_step, 0)

    fresh_count = new_keys.shape[0]
    fresh_k = new_keys[...]
    fresh_v = new_values[...]
    diag = iota((ROWS, HD), 0) == lax.rem(iota((ROWS, HD), 1), ROWS)

    def fresh_scores(request, q):
        s = dot(q, fresh_k, NT) * scale
        row = iota((ROWS, fresh_count), 0)
        col = iota((ROWS, fresh_count), 1)
        live = (lax.div(col, STEPS) == request) & (lax.rem(col, STEPS) <= lax.rem(row, STEPS))
        return jnp.where(live, s, LOW)

    def as_row(column):
        return jnp.sum(jnp.where(diag, column, 0.0), axis=0, keepdims=True)

    quarter = lax.div(iota((1, HD), 1), ROWS)
    for n in range(NEW):
        s = fresh_scores(RES + n, queries[pl.ds((RES + n) * ROWS, ROWS), :])
        m = jnp.max(s, axis=1, keepdims=True)
        p = jnp.exp(s - m)
        l = jnp.sum(p, axis=1, keepdims=True)
        fin[n, 8] = (dot(p.astype(jnp.bfloat16), fresh_v) / l).astype(jnp.bfloat16)
        for g in range(9, GROUPS):
            fin[n, g] = jnp.zeros((ROWS, HD), jnp.bfloat16)
        lf[NZ, pl.ds(n, 1), :] = jnp.where(quarter == 0, as_row(m + jnp.log(l)), LOW)

    loads[0].wait()
    loads[1].wait()
    context = rk.shape[1]

    def resident_step(i, carry):
        for half in range(2):
            request = 2 * i + half
            q = queries[pl.ds(pl.multiple_of(request * ROWS, ROWS), ROWS), :]
            s = dot(q, rk[request], NT) * scale
            s = jnp.where(iota((ROWS, context), 1) < res_len[me * RES + request], s, LOW)
            f = fresh_scores(request, q)
            m = jnp.maximum(
                jnp.max(s, axis=1, keepdims=True), jnp.max(f, axis=1, keepdims=True)
            )
            p = jnp.exp(s - m)
            g = jnp.exp(f - m)
            l = jnp.sum(p, axis=1, keepdims=True) + jnp.sum(g, axis=1, keepdims=True)
            o = dot(p.astype(jnp.bfloat16), rv[request]) + dot(g.astype(jnp.bfloat16), fresh_v)
            att[pl.ds(pl.multiple_of(request * ROWS, ROWS), ROWS), :] = (o / l).astype(
                jnp.bfloat16
            )
        return carry

    lax.fori_loop(0, RES // 2, resident_step, 0)
    partners = [
        inst_at(x, z, y + 1 - 2 * lax.rem(y, 2)),
        inst_at(x, z, lax.rem(y + 2, NY)),
    ]
    mig_copies = []
    for bit in range(2):
        copy = remote(
            att.at[pl.ds((RES - MIG) * ROWS, MIG * ROWS)],
            guest.at[bit],
            mig_send.at[bit],
            mig_recv.at[bit],
            partners[bit],
        )
        copy.start()
        mig_copies.append(copy)

    loads[2].wait()
    loads[3].wait()
    low_half = lax.rem(lax.div(iota((1, HD), 1), ROWS), 2) == 0
    tile_row = iota((2 * NEW, HD), 0)
    key_lane = iota((ROWS, PAGE), 1)

    def partial_step(ip, carry):
        tiles = [jnp.full((2 * NEW, HD), LOW, jnp.float32) for _ in range(PEERS)]
        for half in range(2):
            i = 2 * ip + half
            drain(q2.at[i, pl.ds(1, PEERS - 1)], q2_recv.at[i])
            dest_z = lax.rem(z + order(i), NZ)
            for base in range(0, PEERS, 2):
                scores, values, request = [], [], []
                for r in (base, base + 1):
                    dest = plane(r, dest_z)
                    for c in range(2):
                        at = tab[dest, c]
                        page = tab[dest, 2 * PEERS + c]
                        n = lax.div(at, NPAGES)
                        length = new_len[dest * NEW + jnp.minimum(n, NEW - 1)]
                        live = length - lax.rem(at, NPAGES) * PAGE
                        s = dot(q2[i, r, pl.ds(c * ROWS, ROWS), :], pk[page], NT) * scale
                        scores.append(jnp.where(key_lane < live, s, LOW))
                        values.append(pv[page])
                        request.append(n)
                tops = [jnp.max(s, axis=1, keepdims=True) for s in scores]
                exps = [jnp.exp(s - m) for s, m in zip(scores, tops)]
                sums = [jnp.sum(p, axis=1, keepdims=True) for p in exps]
                outs = [
                    (dot(p.astype(jnp.bfloat16), v) / l).astype(jnp.bfloat16)
                    for p, v, l in zip(exps, values, sums)
                ]
                rows = [as_row(m + jnp.log(l)) for m, l in zip(tops, sums)]
                for k, r in enumerate((base, base + 1)):
                    for c in range(2):
                        if r == 0:
                            r1[i, 0, pl.ds(c * ROWS, ROWS), :] = outs[2 * k + c]
                        else:
                            r1s[i, r, pl.ds(c * ROWS, ROWS), :] = outs[2 * k + c]
                    level = jnp.where(low_half, rows[2 * k], rows[2 * k + 1])
                    wanted = jnp.where(low_half, request[2 * k], request[2 * k + 1]) + half * NEW
                    filled = jnp.where(low_half, request[2 * k], request[2 * k + 1]) < NEW
                    tiles[r] = jnp.where((tile_row == wanted) & filled, level, tiles[r])
                    if r > 0:
                        remote(
                            r1s.at[i, r],
                            r1.at[i, mirror(r)],
                            r1_send.at[i],
                            r1_recv.at[i],
                            plane(r, z),
                        ).start()
        for r in range(PEERS):
            if r == 0:
                st[ip, 0] = tiles[0]
            else:
                sts[ip, r] = tiles[r]
                remote(
                    sts.at[ip, r],
                    st.at[ip, mirror(r)],
                    st_send.at[ip],
                    st_recv.at[ip],
                    plane(r, z),
                ).start()
        return carry

    lax.fori_loop(0, NZ // 2, partial_step, 0)

    for copy in mig_copies:
        copy.wait()
    bit = partner_bit[me]
    hand_here = migrate_out[me]
    hand_there = lax.select(bit == 0, migrate_out[partners[0]], migrate_out[partners[1]])
    nothing = jnp.zeros((ROWS, HD), jnp.bfloat16)
    for r in range(RES):
        attm[pl.ds(r * ROWS, ROWS), :] = lax.select(
            r < RES - hand_here, att[pl.ds(r * ROWS, ROWS), :], nothing
        )
    for m in range(MIG):
        came = lax.select(
            bit == 0, guest[0, pl.ds(m * ROWS, ROWS), :], guest[1, pl.ds(m * ROWS, ROWS), :]
        )
        attm[pl.ds((RES + m) * ROWS, ROWS), :] = lax.select(
            m >= MIG - hand_there, came, nothing
        )

    def by_head(values, slots):
        size = slots * ROWS
        row = iota((size, size), 0)
        col = iota((size, size), 1)
        goal = (
            lax.rem(lax.div(row, STEPS), slots) * ROWS
            + lax.div(row, STEPS * slots) * STEPS
            + lax.rem(row, STEPS)
        )
        moved = dot(jnp.where(col == goal, 1.0, 0.0).astype(jnp.bfloat16), values)
        return moved.astype(jnp.bfloat16)

    moved = by_head(attm[...], RES + MIG)
    lead = (RES + MIG) * STEPS
    for h in range(ROWS // STEPS):
        xres[:, pl.ds(h * HD, HD)] = moved[h * lead : (h + 1) * lead]
    loads[4].wait()
    width = out.shape[1]

    def project(rows_ref, sends, send_sem, recv, recv_sem, own):
        copies = []
        for o in (3, 2, 1, 0):
            peer = tp_peer(o)
            part = dot(rows_ref[...], wv[:, pl.ds(pl.multiple_of(peer * width, width), width)])
            if o == 0:
                own[...] = part
            else:
                sends[o] = part.astype(jnp.bfloat16)
                copy = remote(sends.at[o], recv.at[o], send_sem.at[o], recv_sem.at[o], me, peer)
                copy.start()
                copies.append(copy)
        return copies

    rs1_copies = project(xres, rs1s, rs1_send, rs1, rs1_recv, own1)

    low = iota((2 * NEW, HD), 1) < 2 * ROWS

    def merge(ip, home):
        drain(st.at[ip, pl.ds(1, PEERS - 1)], st_recv.at[ip])
        levels = [
            jnp.where(low, st[ip, 2 * q], st[ip, 2 * q + 1]) for q in range(PEERS // 2)
        ]
        m = jnp.maximum(
            jnp.maximum(levels[0], levels[1]), jnp.maximum(levels[2], levels[3])
        )
        m = jnp.maximum(m, pltpu.roll(m, 2 * ROWS, 1))
        m = jnp.maximum(m, pltpu.roll(m, ROWS, 1))
        shares = [jnp.exp(level - m) for level in levels]
        total = (shares[0] + shares[1]) + (shares[2] + shares[3])
        total = total + pltpu.roll(total, 2 * ROWS, 1)
        total = total + pltpu.roll(total, ROWS, 1)
        ls[ip] = m + jnp.log(total)
        shares = [share / total for share in shares]
        for half in range(2):
            i = 2 * ip + half
            drain(r1.at[i, pl.ds(1, PEERS - 1)], r1_recv.at[i])
            blocks = []
            for n in range(NEW):
                k = half * NEW + n
                blocks.append(
                    jnp.concatenate(
                        [jnp.where(diag, share[k : k + 1], 0.0) for share in shares], axis=1
                    )
                )
            mix = jnp.concatenate(blocks, axis=0).astype(jnp.bfloat16)
            merged = dot(mix, r1[i].reshape(PEERS * 2 * ROWS, HD)).astype(jnp.bfloat16)
            if home and half == 0:
                for n in range(NEW):
                    fin[n, 0] = merged[n * ROWS : (n + 1) * ROWS]
                lf[0] = ls[ip]
            else:
                for n in range(NEW):
                    r2s[i, n] = merged[n * ROWS : (n + 1) * ROWS]
                zi = order(i)
                turned = i + 1 - 2 * lax.rem(i + 1, 2)
                back = turned - lax.div(turned, NZ)
                remote(
                    r2s.at[i], fin.at[:, back], r2_send.at[i], r2_recv.at[back], line(zi)
                ).start()
                remote(ls.at[ip], lf.at[back], lf_send.at[i], lf_recv.at[back], line(zi)).start()

    merge(jnp.int32(0), True)

    def merge_step(ip, carry):
        merge(ip, False)
        return carry

    lax.fori_loop(1, NZ // 2, merge_step, 0)

    for i in range(1, NZ):
        drain(lf.at[i], lf_recv.at[i])
        drain(fin.at[:, i], r2_recv.at[i])
    from_odd = [False, False, True, False, True, False, True, True]
    levels = []
    for base in range(0, NZ, 4):
        level = jnp.full((NEW, HD), LOW, jnp.float32)
        for g in range(4):
            i = base + g
            rows = lf[i, pl.ds(NEW if from_odd[i] else 0, NEW), :]
            level = jnp.where(quarter == g, rows, level)
        levels.append(level)
    levels.append(lf[NZ, pl.ds(0, NEW), :])
    m = jnp.maximum(jnp.maximum(levels[0], levels[1]), levels[2])
    m = jnp.maximum(m, pltpu.roll(m, 2 * ROWS, 1))
    m = jnp.maximum(m, pltpu.roll(m, ROWS, 1))
    shares = [jnp.exp(level - m) for level in levels]
    total = shares[0] + shares[1] + shares[2]
    total = total + pltpu.roll(total, 2 * ROWS, 1)
    total = total + pltpu.roll(total, ROWS, 1)
    shares = [share / total for share in shares]
    attended = []
    for n in range(NEW):
        mix = jnp.concatenate(
            [jnp.where(diag, share[n : n + 1], 0.0) for share in shares], axis=1
        ).astype(jnp.bfloat16)
        attended.append(dot(mix, fin[n].reshape(GROUPS * ROWS, HD)))
    moved = by_head(jnp.concatenate(attended, axis=0).astype(jnp.bfloat16), NEW)
    tail = NEW * STEPS
    for h in range(ROWS // STEPS):
        xnew[:, pl.ds(h * HD, HD)] = moved[h * tail : (h + 1) * tail]
    rs2_copies = project(xnew, rs2s, rs2_send, rs2, rs2_recv, own2)

    for copy in rs1_copies:
        copy.wait()
    total = own1[...]
    for o in range(1, TP):
        total = total + rs1[o].astype(jnp.float32)
    out[pl.ds(0, lead), :] = total.astype(jnp.bfloat16)
    for copy in q1_copies:
        copy.wait_send()
    for i in range(NZ):
        drain(fw.at[i, pl.ds(1, PEERS - 1)], q2_send.at[i])
        drain(r1s.at[i, pl.ds(1, PEERS - 1)], r1_send.at[i])
        if i > 0:
            drain(r2s.at[i], r2_send.at[i])
            drain(ls.at[i // 2], lf_send.at[i])
    for ip in range(NZ // 2):
        drain(sts.at[ip, pl.ds(1, PEERS - 1)], st_send.at[ip])
    for copy in rs2_copies:
        copy.wait()
    total = own2[...]
    for o in range(1, TP):
        total = total + rs2[o].astype(jnp.float32)
    out[pl.ds(lead, tail), :] = total.astype(jnp.bfloat16)


def per_device(
    res_keys,
    res_values,
    pool_keys,
    pool_values,
    queries,
    new_keys,
    new_values,
    res_len,
    new_len,
    page_source,
    page_index,
    partner_bit,
    migrate_out,
    out_weight,
):
    bf, f32 = jnp.bfloat16, jnp.float32
    rows = (RES + MIG + NEW) * STEPS
    lead, tail = (RES + MIG) * STEPS, NEW * STEPS
    width = out_weight.shape[1] // TP
    smem = pl.BlockSpec(memory_space=pltpu.SMEM)
    vmem = pl.BlockSpec(memory_space=pltpu.VMEM)
    hbm = pl.BlockSpec(memory_space=pl.ANY)
    dma = pltpu.SemaphoreType.DMA
    depth = out_weight.shape[0]
    scratch = [
        pltpu.VMEM((RES, res_keys.shape[2], HD), bf),
        pltpu.VMEM((RES, res_keys.shape[2], HD), bf),
        pltpu.VMEM((pool_keys.shape[0], PAGE, HD), bf),
        pltpu.VMEM((pool_keys.shape[0], PAGE, HD), bf),
        pltpu.VMEM(out_weight.shape, bf),
        pltpu.VMEM((page_source.shape[0], HD), jnp.int32),
        pltpu.SMEM((page_source.shape[0], HD), jnp.int32),
        pltpu.VMEM((NZ, NEW * ROWS, HD), bf),
        pltpu.VMEM((NZ, PEERS, 2 * ROWS, HD), bf),
        pltpu.VMEM((NZ, PEERS, 2 * ROWS, HD), bf),
        pltpu.VMEM((NZ, PEERS, 2 * ROWS, HD), bf),
        pltpu.VMEM((NZ, PEERS, 2 * ROWS, HD), bf),
        pltpu.VMEM((NZ // 2, PEERS, 2 * NEW, HD), f32),
        pltpu.VMEM((NZ // 2, PEERS, 2 * NEW, HD), f32),
        pltpu.VMEM((NZ, NEW, ROWS, HD), bf),
        pltpu.VMEM((NZ // 2, 2 * NEW, HD), f32),
        pltpu.VMEM((NEW, GROUPS, ROWS, HD), bf),
        pltpu.VMEM((NZ + 1, 2 * NEW, HD), f32),
        pltpu.VMEM((RES * ROWS, HD), bf),
        pltpu.VMEM((2, MIG * ROWS, HD), bf),
        pltpu.VMEM(((RES + MIG) * ROWS, HD), bf),
        pltpu.VMEM((lead, depth), bf),
        pltpu.VMEM((tail, depth), bf),
        pltpu.VMEM((lead, width), f32),
        pltpu.VMEM((tail, width), f32),
        pltpu.VMEM((TP, lead, width), bf),
        pltpu.VMEM((TP, lead, width), bf),
        pltpu.VMEM((TP, tail, width), bf),
        pltpu.VMEM((TP, tail, width), bf),
        dma((6,)),
        dma((NZ,)),
        dma((NZ,)),
        dma((NZ,)),
        dma((NZ,)),
        dma((NZ,)),
        dma((NZ,)),
        dma((NZ // 2,)),
        dma((NZ // 2,)),
        dma((NZ,)),
        dma((NZ,)),
        dma((NZ,)),
        dma((NZ,)),
        dma((2,)),
        dma((2,)),
        dma((TP,)),
        dma((TP,)),
        dma((TP,)),
        dma((TP,)),
    ]
    return pl.pallas_call(
        kernel,
        out_shape=jax.ShapeDtypeStruct((rows, width), bf),
        in_specs=[smem] * 4 + [vmem] * 5 + [hbm] * 5,
        out_specs=vmem,
        scratch_shapes=scratch,
        compiler_params=pltpu.CompilerParams(
            collective_id=0, has_side_effects=True, vmem_limit_bytes=48 * 2**20
        ),
        cost_estimate=pl.CostEstimate(
            flops=10**9, bytes_accessed=16 * 2**20, transcendentals=10**6
        ),
    )(
        res_len,
        new_len,
        partner_bit,
        migrate_out,
        page_source,
        page_index,
        queries.reshape(-1, HD),
        new_keys.reshape(-1, HD),
        new_values.reshape(-1, HD),
        res_keys.reshape(RES, -1, HD),
        res_values.reshape(RES, -1, HD),
        pool_keys.reshape(-1, PAGE, HD),
        pool_values.reshape(-1, PAGE, HD),
        out_weight,
    )


def solution(mesh):
    heads = P("inst", "tp", None, None)
    in_specs = (heads,) * 7 + (P(),) * 6 + (P("tp", None),)
    return jax.shard_map(
        per_device, mesh=mesh, in_specs=in_specs, out_specs=P("inst", "tp"), check_vma=False
    )
```

```python
import math

import jax
import jax.numpy as jnp
from jax import lax
from jax.experimental import pallas as pl
from jax.experimental.pallas import tpu as pltpu
from jax.sharding import PartitionSpec as P

MESH = pl.DeviceIdType.MESH
NX, NZ, NY = 2, 8, 4
PEERS = NX * NY
TP = 4
RES, NEW, MIG = 6, 4, 2
STEPS = 4
ROWS = 32
HD = 128
PAGE = 128
NPAGES = 16
LOW = -1e30
NT = (((1,), (1,)), ((), ()))
NN = (((1,), (0,)), ((), ()))


def mirror(r):
    dx, dy = divmod(r, NY)
    return dx * NY + (NY - dy) % NY


def iota(shape, axis):
    return lax.broadcasted_iota(jnp.int32, shape, axis)


def dot(a, b, dims=NN):
    return lax.dot_general(a, b, dims, preferred_element_type=jnp.float32)


def kernel(
    res_len_in,
    new_len_in,
    partner_bit_in,
    migrate_out_in,
    page_source_in,
    page_index_in,
    queries_in,
    new_keys_in,
    new_values_in,
    res_keys,
    res_values,
    pool_keys,
    pool_values,
    weight,
    out,
    res_len,
    new_len,
    partner_bit,
    migrate_out,
    page_source,
    page_index,
    queries,
    new_keys,
    new_values,
    rk,
    rv,
    pk,
    pv,
    wv,
    tab_v,
    tab,
    q1,
    fw,
    q2,
    r1s,
    r1,
    sts,
    st,
    r2s,
    ls,
    fin,
    lf,
    att,
    guest,
    attm,
    xres,
    xnew,
    own1,
    own2,
    rs1s,
    rs1,
    rs2s,
    rs2,
    load_sem,
    q1_send,
    q1_recv,
    q2_send,
    q2_recv,
    r1_send,
    r1_recv,
    st_send,
    st_recv,
    r2_send,
    r2_recv,
    lf_send,
    lf_recv,
    mig_send,
    mig_recv,
    rs1_send,
    rs1_recv,
    rs2_send,
    rs2_recv,
):
    me = lax.axis_index("inst")
    tp = lax.axis_index("tp")
    y = lax.rem(me, NY)
    z = lax.rem(lax.div(me, NY), NZ)
    x = lax.div(me, NY * NZ)
    hi = lax.div(tp, 2)
    core = lax.rem(tp, 2)
    scale = 1.0 / math.sqrt(HD)

    def inst_at(xx, zz, yy):
        return (xx * NZ + zz) * NY + yy

    def plane(r, zz):
        dx, dy = divmod(r, NY)
        return inst_at(lax.rem(x + dx, NX), zz, lax.rem(y + dy, NY))

    def line(zi):
        return inst_at(x, lax.rem(z + zi, NZ), y)

    def tp_peer(o):
        return lax.rem(hi + o // 2, 2) * 2 + lax.rem(core + o % 2, 2)

    def order(i):
        odd = lax.rem(i, 2)
        return lax.rem(odd * lax.div(i + 1, 2) + (1 - odd) * (NZ - lax.div(i, 2)), NZ)

    def remote(src, dst, send, recv, inst, t=tp):
        return pltpu.make_async_remote_copy(
            src_ref=src,
            dst_ref=dst,
            send_sem=send,
            recv_sem=recv,
            device_id=(inst, t),
            device_id_type=MESH,
        )

    def drain(ref, sem):
        pltpu.make_async_copy(ref, ref, sem).wait()

    loads = [
        pltpu.make_async_copy(src, dst, load_sem.at[k])
        for k, (src, dst) in enumerate(
            [
                (res_keys, rk),
                (res_values, rv),
                (pool_keys, pk),
                (pool_values, pv),
                (weight, wv),
                (page_source_in, page_source),
                (page_index_in, page_index),
                (queries_in, queries),
                (new_keys_in, new_keys),
                (new_values_in, new_values),
                (res_len_in, res_len),
                (new_len_in, new_len),
                (partner_bit_in, partner_bit),
                (migrate_out_in, migrate_out),
            ]
        )
    ]
    for k in (5, 6, 7, 11, 10, 8, 9, 12, 13, 0, 1, 2, 3, 4):
        loads[k].start()

    barrier = pltpu.get_barrier_semaphore()
    for zi in range(1, NZ):
        pl.semaphore_signal(barrier, inc=1, device_id=(line(zi), tp), device_id_type=MESH)
    for r in range(1, PEERS):
        pl.semaphore_signal(barrier, inc=1, device_id=(plane(r, z), tp), device_id_type=MESH)
    for o in range(1, TP):
        pl.semaphore_signal(barrier, inc=1, device_id=(me, tp_peer(o)), device_id_type=MESH)
    loads[5].wait()
    loads[6].wait()
    places = page_source.shape[1]
    count = page_source.shape[0]
    source = page_source[...]
    slot = page_index[...]
    place = iota((count, places), 1)
    lane = iota((count, HD), 1)
    table = jnp.zeros((count, HD), jnp.int32)
    for r in range(PEERS):
        hit = source == plane(r, z)
        first = jnp.min(jnp.where(hit, place, places), axis=1, keepdims=True)
        last = jnp.max(jnp.where(hit, place, -1), axis=1, keepdims=True)
        last = jnp.where(last > first, last, places)
        table = jnp.where(lane == 2 * r, first, table)
        table = jnp.where(lane == 2 * r + 1, last, table)
        if r == 0:
            for c, p in ((0, first), (1, last)):
                page = jnp.max(jnp.where(place == p, slot, 0), axis=1, keepdims=True)
                table = jnp.where(lane == 2 * PEERS + c, page, table)
    tab_v[...] = table
    tab_copy = pltpu.make_async_copy(tab_v, tab, load_sem.at[14])
    tab_copy.start()

    pl.semaphore_wait(barrier, NZ - 1 + PEERS - 1 + TP - 1)

    seq = [0, 1, 7, 2, 6, 3, 5, 4]
    q1_copies = []
    loads[7].wait()
    for i in range(1, NZ):
        zi = seq[i]
        back = seq.index(NZ - zi)
        copy = remote(
            queries.at[pl.ds(RES * ROWS, NEW * ROWS)],
            q1.at[back],
            q1_send.at[i],
            q1_recv.at[back],
            line(zi),
        )
        copy.start()
        q1_copies.append(copy)
    q1[0] = queries[RES * ROWS :, :]

    def forward(i):
        dest = line(order(i))
        block = [q1[i, pl.ds(n * ROWS, ROWS), :] for n in range(NEW)]
        for r in range(PEERS):
            for c in range(2):
                n = lax.div(tab[dest, 2 * r + c], NPAGES)
                q = lax.select(
                    n == 0,
                    block[0],
                    lax.select(n == 1, block[1], lax.select(n == 2, block[2], block[3])),
                )
                if r == 0:
                    q2[i, 0, pl.ds(c * ROWS, ROWS), :] = q
                else:
                    fw[i, r, pl.ds(c * ROWS, ROWS), :] = q
            if r > 0:
                remote(
                    fw.at[i, r], q2.at[i, mirror(r)], q2_send.at[i], q2_recv.at[i], plane(r, z)
                ).start()

    tab_copy.wait()
    forward(jnp.int32(0))

    def forward_step(i, carry):
        drain(q1.at[i], q1_recv.at[i])
        forward(i)
        return carry

    lax.fori_loop(1, NZ, forward_step, 0)

    for k in range(8, 14):
        loads[k].wait()
    fresh_count = new_keys.shape[0]
    fresh_k = new_keys[...]
    fresh_v = new_values[...]
    diag = iota((ROWS, HD), 0) == lax.rem(iota((ROWS, HD), 1), ROWS)

    def fresh_scores(request, q):
        s = dot(q, fresh_k, NT) * scale
        row = iota((ROWS, fresh_count), 0)
        col = iota((ROWS, fresh_count), 1)
        live = (lax.div(col, STEPS) == request) & (lax.rem(col, STEPS) <= lax.rem(row, STEPS))
        return jnp.where(live, s, LOW)

    def as_row(column):
        return jnp.sum(jnp.where(diag, column, 0.0), axis=0, keepdims=True)

    quarter = lax.div(iota((1, HD), 1), ROWS)
    for n in range(NEW):
        s = fresh_scores(RES + n, queries[pl.ds((RES + n) * ROWS, ROWS), :])
        m = jnp.max(s, axis=1, keepdims=True)
        p = jnp.exp(s - m)
        l = jnp.sum(p, axis=1, keepdims=True)
        fin[n, 0] = (dot(p.astype(jnp.bfloat16), fresh_v) / l).astype(jnp.bfloat16)
        lf[0, pl.ds(n, 1), :] = as_row(m + jnp.log(l))

    loads[0].wait()
    loads[1].wait()
    context = rk.shape[1]

    def resident_step(i, carry):
        for half in range(2):
            request = 2 * i + half
            q = queries[pl.ds(pl.multiple_of(request * ROWS, ROWS), ROWS), :]
            s = dot(q, rk[request], NT) * scale
            s = jnp.where(iota((ROWS, context), 1) < res_len[me * RES + request], s, LOW)
            f = fresh_scores(request, q)
            m = jnp.maximum(
                jnp.max(s, axis=1, keepdims=True), jnp.max(f, axis=1, keepdims=True)
            )
            p = jnp.exp(s - m)
            g = jnp.exp(f - m)
            l = jnp.sum(p, axis=1, keepdims=True) + jnp.sum(g, axis=1, keepdims=True)
            o = dot(p.astype(jnp.bfloat16), rv[request]) + dot(g.astype(jnp.bfloat16), fresh_v)
            att[pl.ds(pl.multiple_of(request * ROWS, ROWS), ROWS), :] = (o / l).astype(
                jnp.bfloat16
            )
        return carry

    lax.fori_loop(0, RES // 2, resident_step, 0)
    partners = [
        inst_at(x, z, y + 1 - 2 * lax.rem(y, 2)),
        inst_at(x, z, lax.rem(y + 2, NY)),
    ]
    mig_copies = []
    for bit in range(2):
        copy = remote(
            att.at[pl.ds((RES - MIG) * ROWS, MIG * ROWS)],
            guest.at[bit],
            mig_send.at[bit],
            mig_recv.at[bit],
            partners[bit],
        )
        copy.start()
        mig_copies.append(copy)

    loads[2].wait()
    loads[3].wait()
    low_half = lax.rem(lax.div(iota((1, HD), 1), ROWS), 2) == 0
    tile_row = iota((2 * NEW, HD), 0)
    key_lane = iota((ROWS, PAGE), 1)

    def send_part(i, r):
        remote(
            r1s.at[i, r], r1.at[i, mirror(r)], r1_send.at[i], r1_recv.at[i], plane(r, z)
        ).start()

    def send_level(ip, r):
        remote(
            sts.at[ip, r], st.at[ip, mirror(r)], st_send.at[ip], st_recv.at[ip], plane(r, z)
        ).start()

    def partial_pair(ip, send):
        tiles = [jnp.full((2 * NEW, HD), LOW, jnp.float32) for _ in range(PEERS)]
        for half in range(2):
            i = 2 * ip + half
            drain(q2.at[i, pl.ds(1, PEERS - 1)], q2_recv.at[i])
            dest_z = lax.rem(z + order(i), NZ)
            for base in range(0, PEERS, 2):
                scores, values, request = [], [], []
                for r in (base, base + 1):
                    dest = plane(r, dest_z)
                    for c in range(2):
                        at = tab[dest, c]
                        page = tab[dest, 2 * PEERS + c]
                        n = lax.div(at, NPAGES)
                        length = new_len[dest * NEW + jnp.minimum(n, NEW - 1)]
                        live = length - lax.rem(at, NPAGES) * PAGE
                        s = dot(q2[i, r, pl.ds(c * ROWS, ROWS), :], pk[page], NT) * scale
                        scores.append(jnp.where(key_lane < live, s, LOW))
                        values.append(pv[page])
                        request.append(n)
                tops = [jnp.max(s, axis=1, keepdims=True) for s in scores]
                exps = [jnp.exp(s - m) for s, m in zip(scores, tops)]
                sums = [jnp.sum(p, axis=1, keepdims=True) for p in exps]
                outs = [
                    (dot(p.astype(jnp.bfloat16), v) / l).astype(jnp.bfloat16)
                    for p, v, l in zip(exps, values, sums)
                ]
                rows = [as_row(m + jnp.log(l)) for m, l in zip(tops, sums)]
                for k, r in enumerate((base, base + 1)):
                    for c in range(2):
                        if r == 0:
                            r1[i, 0, pl.ds(c * ROWS, ROWS), :] = outs[2 * k + c]
                        else:
                            r1s[i, r, pl.ds(c * ROWS, ROWS), :] = outs[2 * k + c]
                    level = jnp.where(low_half, rows[2 * k], rows[2 * k + 1])
                    wanted = jnp.where(low_half, request[2 * k], request[2 * k + 1]) + half * NEW
                    filled = jnp.where(low_half, request[2 * k], request[2 * k + 1]) < NEW
                    tiles[r] = jnp.where((tile_row == wanted) & filled, level, tiles[r])
                    if r > 0 and send:
                        send_part(i, r)
        for r in range(PEERS):
            if r == 0:
                st[ip, 0] = tiles[0]
            else:
                sts[ip, r] = tiles[r]
                if send:
                    send_level(ip, r)

    def partial_step(ip, carry):
        partial_pair(ip, True)
        return carry

    partial_pair(jnp.int32(0), False)
    lax.fori_loop(1, NZ // 2, partial_step, 0)
    for r in range(1, PEERS):
        send_level(0, r)
    for i in (1, 0):
        for r in range(1, PEERS):
            send_part(i, r)

    for copy in mig_copies:
        copy.wait()
    bit = partner_bit[me]
    hand_here = migrate_out[me]
    hand_there = lax.select(bit == 0, migrate_out[partners[0]], migrate_out[partners[1]])
    nothing = jnp.zeros((ROWS, HD), jnp.bfloat16)
    for r in range(RES):
        attm[pl.ds(r * ROWS, ROWS), :] = lax.select(
            r < RES - hand_here, att[pl.ds(r * ROWS, ROWS), :], nothing
        )
    for m in range(MIG):
        came = lax.select(
            bit == 0, guest[0, pl.ds(m * ROWS, ROWS), :], guest[1, pl.ds(m * ROWS, ROWS), :]
        )
        attm[pl.ds((RES + m) * ROWS, ROWS), :] = lax.select(
            m >= MIG - hand_there, came, nothing
        )

    def by_head(values, slots):
        size = slots * ROWS
        row = iota((size, size), 0)
        col = iota((size, size), 1)
        goal = (
            lax.rem(lax.div(row, STEPS), slots) * ROWS
            + lax.div(row, STEPS * slots) * STEPS
            + lax.rem(row, STEPS)
        )
        moved = dot(jnp.where(col == goal, 1.0, 0.0).astype(jnp.bfloat16), values)
        return moved.astype(jnp.bfloat16)

    moved = by_head(attm[...], RES + MIG)
    lead = (RES + MIG) * STEPS
    for h in range(ROWS // STEPS):
        xres[:, pl.ds(h * HD, HD)] = moved[h * lead : (h + 1) * lead]
    loads[4].wait()
    width = out.shape[1]

    def project(rows_ref, sends, send_sem, recv, recv_sem, own):
        copies = []
        for o in (3, 2, 1, 0):
            peer = tp_peer(o)
            part = dot(rows_ref[...], wv[:, pl.ds(pl.multiple_of(peer * width, width), width)])
            if o == 0:
                own[...] = part
            else:
                sends[o] = part.astype(jnp.bfloat16)
                copy = remote(sends.at[o], recv.at[o], send_sem.at[o], recv_sem.at[o], me, peer)
                copy.start()
                copies.append(copy)
        return copies

    rs1_copies = project(xres, rs1s, rs1_send, rs1, rs1_recv, own1)

    low = iota((2 * NEW, HD), 1) < 2 * ROWS

    def pair_levels(ip):
        drain(st.at[ip, pl.ds(1, PEERS - 1)], st_recv.at[ip])
        return [
            jnp.where(low, st[ip, 2 * q], st[ip, 2 * q + 1]) for q in range(PEERS // 2)
        ]

    def softmax_over(levels):
        m = levels[0]
        for level in levels[1:]:
            m = jnp.maximum(m, level)
        m = jnp.maximum(m, pltpu.roll(m, 2 * ROWS, 1))
        m = jnp.maximum(m, pltpu.roll(m, ROWS, 1))
        shares = [jnp.exp(level - m) for level in levels]
        total = shares[0]
        for share in shares[1:]:
            total = total + share
        total = total + pltpu.roll(total, 2 * ROWS, 1)
        total = total + pltpu.roll(total, ROWS, 1)
        return [share / total for share in shares], m + jnp.log(total)

    def merge(ip, levels, halves):
        shares, together = softmax_over(levels)
        ls[ip] = together
        for half in halves:
            i = 2 * ip + half
            drain(r1.at[i, pl.ds(1, PEERS - 1)], r1_recv.at[i])
            blocks = []
            for n in range(NEW):
                k = half * NEW + n
                blocks.append(
                    jnp.concatenate(
                        [jnp.where(diag, share[k : k + 1], 0.0) for share in shares], axis=1
                    )
                )
            mix = jnp.concatenate(blocks, axis=0).astype(jnp.bfloat16)
            merged = dot(mix, r1[i].reshape(PEERS * 2 * ROWS, HD)).astype(jnp.bfloat16)
            for n in range(NEW):
                r2s[i, n] = merged[n * ROWS : (n + 1) * ROWS]
            zi = order(i)
            turned = i + 1 - 2 * lax.rem(i + 1, 2)
            back = turned - lax.div(turned, NZ)
            remote(
                r2s.at[i], fin.at[:, back], r2_send.at[i], r2_recv.at[back], line(zi)
            ).start()
            remote(ls.at[ip], lf.at[back], lf_send.at[i], lf_recv.at[back], line(zi)).start()

    def merge_step(ip, carry):
        merge(ip, pair_levels(ip), (0, 1))
        return carry

    lax.fori_loop(1, NZ // 2, merge_step, 0)
    near = pair_levels(0)
    merge(jnp.int32(0), near, (1,))

    for i in range(1, NZ):
        drain(lf.at[i], lf_recv.at[i])
        drain(fin.at[:, i], r2_recv.at[i])
    from_odd = [False, False, True, False, True, False, True, True]
    levels = [level[:NEW] for level in near]
    for base in range(0, NZ, 4):
        level = jnp.full((NEW, HD), LOW, jnp.float32)
        for g in range(4):
            i = base + g
            rows = lf[i, pl.ds(NEW if from_odd[i] else 0, NEW), :]
            level = jnp.where(quarter == g, rows, level)
        levels.append(level)
    shares, _ = softmax_over(levels)
    tail = NEW * STEPS
    row = iota((tail, HD), 0)
    spread = []
    for share in shares:
        wide = jnp.zeros((tail, HD), jnp.float32)
        for n in range(NEW):
            wide = jnp.where(lax.div(row, STEPS) == n, share[n : n + 1], wide)
        spread.append(wide)
    column = lax.rem(iota((tail, HD), 1), ROWS) - lax.rem(row, STEPS)
    owner = lax.div(row, STEPS)

    def mixing(parts, n):
        rows = []
        for h in range(ROWS // STEPS):
            keep = column == h * STEPS
            if n is not None:
                keep = keep & (owner == n)
            rows.append(
                jnp.concatenate([jnp.where(keep, part, 0.0) for part in parts], axis=1)
            )
        return jnp.concatenate(rows, axis=0).astype(jnp.bfloat16)

    drain(r1.at[0, pl.ds(1, PEERS - 1)], r1_recv.at[0])
    attended = dot(mixing(spread[: PEERS // 2], None), r1[0].reshape(PEERS * 2 * ROWS, HD))
    for n in range(NEW):
        attended = attended + dot(
            mixing(spread[PEERS // 2 :], n), fin[n].reshape(NZ * ROWS, HD)
        )
    attended = attended.astype(jnp.bfloat16)
    for h in range(ROWS // STEPS):
        xnew[:, pl.ds(h * HD, HD)] = attended[h * tail : (h + 1) * tail]
    rs2_copies = project(xnew, rs2s, rs2_send, rs2, rs2_recv, own2)

    for copy in rs1_copies:
        copy.wait()
    total = own1[...]
    for o in range(1, TP):
        total = total + rs1[o].astype(jnp.float32)
    out[pl.ds(0, lead), :] = total.astype(jnp.bfloat16)
    for copy in q1_copies:
        copy.wait_send()
    for i in range(NZ):
        drain(fw.at[i, pl.ds(1, PEERS - 1)], q2_send.at[i])
        drain(r1s.at[i, pl.ds(1, PEERS - 1)], r1_send.at[i])
        if i > 0:
            drain(r2s.at[i], r2_send.at[i])
            drain(ls.at[i // 2], lf_send.at[i])
    for ip in range(NZ // 2):
        drain(sts.at[ip, pl.ds(1, PEERS - 1)], st_send.at[ip])
    for copy in rs2_copies:
        copy.wait()
    total = own2[...]
    for o in range(1, TP):
        total = total + rs2[o].astype(jnp.float32)
    out[pl.ds(lead, tail), :] = total.astype(jnp.bfloat16)


def per_device(
    res_keys,
    res_values,
    pool_keys,
    pool_values,
    queries,
    new_keys,
    new_values,
    res_len,
    new_len,
    page_source,
    page_index,
    partner_bit,
    migrate_out,
    out_weight,
):
    bf, f32 = jnp.bfloat16, jnp.float32
    rows = (RES + MIG + NEW) * STEPS
    lead, tail = (RES + MIG) * STEPS, NEW * STEPS
    width = out_weight.shape[1] // TP
    vmem = pl.BlockSpec(memory_space=pltpu.VMEM)
    hbm = pl.BlockSpec(memory_space=pltpu.HBM)
    dma = pltpu.SemaphoreType.DMA
    depth = out_weight.shape[0]
    whole = [
        pltpu.SMEM(res_len.shape, jnp.int32),
        pltpu.SMEM(new_len.shape, jnp.int32),
        pltpu.SMEM(partner_bit.shape, jnp.int32),
        pltpu.SMEM(migrate_out.shape, jnp.int32),
        pltpu.VMEM(page_source.shape, jnp.int32),
        pltpu.VMEM(page_index.shape, jnp.int32),
        pltpu.VMEM((queries.shape[0] * ROWS, HD), bf),
        pltpu.VMEM((queries.shape[0] * STEPS, HD), bf),
        pltpu.VMEM((queries.shape[0] * STEPS, HD), bf),
    ]
    scratch = whole + [
        pltpu.VMEM((RES, res_keys.shape[2], HD), bf),
        pltpu.VMEM((RES, res_keys.shape[2], HD), bf),
        pltpu.VMEM((pool_keys.shape[0], PAGE, HD), bf),
        pltpu.VMEM((pool_keys.shape[0], PAGE, HD), bf),
        pltpu.VMEM(out_weight.shape, bf),
        pltpu.VMEM((page_source.shape[0], HD), jnp.int32),
        pltpu.SMEM((page_source.shape[0], HD), jnp.int32),
        pltpu.VMEM((NZ, NEW * ROWS, HD), bf),
        pltpu.VMEM((NZ, PEERS, 2 * ROWS, HD), bf),
        pltpu.VMEM((NZ, PEERS, 2 * ROWS, HD), bf),
        pltpu.VMEM((NZ, PEERS, 2 * ROWS, HD), bf),
        pltpu.VMEM((NZ, PEERS, 2 * ROWS, HD), bf),
        pltpu.VMEM((NZ // 2, PEERS, 2 * NEW, HD), f32),
        pltpu.VMEM((NZ // 2, PEERS, 2 * NEW, HD), f32),
        pltpu.VMEM((NZ, NEW, ROWS, HD), bf),
        pltpu.VMEM((NZ // 2, 2 * NEW, HD), f32),
        pltpu.VMEM((NEW, NZ, ROWS, HD), bf),
        pltpu.VMEM((NZ, 2 * NEW, HD), f32),
        pltpu.VMEM((RES * ROWS, HD), bf),
        pltpu.VMEM((2, MIG * ROWS, HD), bf),
        pltpu.VMEM(((RES + MIG) * ROWS, HD), bf),
        pltpu.VMEM((lead, depth), bf),
        pltpu.VMEM((tail, depth), bf),
        pltpu.VMEM((lead, width), f32),
        pltpu.VMEM((tail, width), f32),
        pltpu.VMEM((TP, lead, width), bf),
        pltpu.VMEM((TP, lead, width), bf),
        pltpu.VMEM((TP, tail, width), bf),
        pltpu.VMEM((TP, tail, width), bf),
        dma((15,)),
        dma((NZ,)),
        dma((NZ,)),
        dma((NZ,)),
        dma((NZ,)),
        dma((NZ,)),
        dma((NZ,)),
        dma((NZ // 2,)),
        dma((NZ // 2,)),
        dma((NZ,)),
        dma((NZ,)),
        dma((NZ,)),
        dma((NZ,)),
        dma((2,)),
        dma((2,)),
        dma((TP,)),
        dma((TP,)),
        dma((TP,)),
        dma((TP,)),
    ]
    return pl.pallas_call(
        kernel,
        out_shape=jax.ShapeDtypeStruct((rows, width), bf),
        in_specs=[hbm] * 14,
        out_specs=vmem,
        scratch_shapes=scratch,
        compiler_params=pltpu.CompilerParams(
            collective_id=0, has_side_effects=True, vmem_limit_bytes=64 * 2**20
        ),
        cost_estimate=pl.CostEstimate(
            flops=10**9, bytes_accessed=16 * 2**20, transcendentals=10**6
        ),
    )(
        res_len,
        new_len,
        partner_bit,
        migrate_out,
        page_source,
        page_index,
        queries.reshape(-1, HD),
        new_keys.reshape(-1, HD),
        new_values.reshape(-1, HD),
        res_keys.reshape(RES, -1, HD),
        res_values.reshape(RES, -1, HD),
        pool_keys.reshape(-1, PAGE, HD),
        pool_values.reshape(-1, PAGE, HD),
        out_weight,
    )


def solution(mesh):
    heads = P("inst", "tp", None, None)
    in_specs = (heads,) * 7 + (P(),) * 6 + (P("tp", None),)
    return jax.shard_map(
        per_device, mesh=mesh, in_specs=in_specs, out_specs=P("inst", "tp"), check_vma=False
    )
```

```python
import math

import jax
import jax.numpy as jnp
from jax import lax
from jax.experimental import pallas as pl
from jax.experimental.pallas import tpu as pltpu
from jax.sharding import PartitionSpec as P

MESH = pl.DeviceIdType.MESH
NX, NZ, NY = 2, 8, 4
PEERS = NX * NY
TP = 4
RES, NEW, MIG = 6, 4, 2
STEPS = 4
ROWS = 32
HD = 128
PAGE = 128
NPAGES = 16
LOW = -1e30
NT = (((1,), (1,)), ((), ()))
NN = (((1,), (0,)), ((), ()))


def mirror(r):
    dx, dy = divmod(r, NY)
    return dx * NY + (NY - dy) % NY


def iota(shape, axis):
    return lax.broadcasted_iota(jnp.int32, shape, axis)


def dot(a, b, dims=NN):
    return lax.dot_general(a, b, dims, preferred_element_type=jnp.float32)


def kernel(
    res_len_in,
    new_len_in,
    partner_bit_in,
    migrate_out_in,
    page_source_in,
    page_index_in,
    queries_in,
    new_keys_in,
    new_values_in,
    res_keys,
    res_values,
    pool_keys,
    pool_values,
    weight,
    out,
    res_len,
    new_len,
    partner_bit,
    migrate_out,
    page_source,
    page_index,
    queries,
    new_keys,
    new_values,
    rk,
    rv,
    pk,
    pv,
    wv,
    tab_v,
    tab,
    q1,
    fw,
    q2,
    r1s,
    r1,
    sts,
    st,
    r2s,
    ls,
    fin,
    lf,
    att,
    guest,
    attm,
    xres,
    xnew,
    own1,
    own2,
    rs1s,
    rs1,
    rs2s,
    rs2,
    load_sem,
    q1_send,
    q1_recv,
    q2_send,
    q2_recv,
    r1_send,
    r1_recv,
    st_send,
    st_recv,
    r2_send,
    r2_recv,
    lf_send,
    lf_recv,
    mig_send,
    mig_recv,
    rs1_send,
    rs1_recv,
    rs2_send,
    rs2_recv,
):
    me = lax.axis_index("inst")
    tp = lax.axis_index("tp")
    y = lax.rem(me, NY)
    z = lax.rem(lax.div(me, NY), NZ)
    x = lax.div(me, NY * NZ)
    hi = lax.div(tp, 2)
    core = lax.rem(tp, 2)
    scale = 1.0 / math.sqrt(HD)

    def inst_at(xx, zz, yy):
        return (xx * NZ + zz) * NY + yy

    def plane(r, zz):
        dx, dy = divmod(r, NY)
        return inst_at(lax.rem(x + dx, NX), zz, lax.rem(y + dy, NY))

    def line(zi):
        return inst_at(x, lax.rem(z + zi, NZ), y)

    bases = [plane(r, 0) for r in range(PEERS)]
    peers = [base + z * NY for base in bases]

    def tp_peer(o):
        return lax.rem(hi + o // 2, 2) * 2 + lax.rem(core + o % 2, 2)

    def order(i):
        odd = lax.rem(i, 2)
        return lax.rem(odd * lax.div(i + 1, 2) + (1 - odd) * (NZ - lax.div(i, 2)), NZ)

    def remote(src, dst, send, recv, inst, t=tp):
        return pltpu.make_async_remote_copy(
            src_ref=src,
            dst_ref=dst,
            send_sem=send,
            recv_sem=recv,
            device_id=(inst, t),
            device_id_type=MESH,
        )

    def drain(ref, sem):
        pltpu.make_async_copy(ref, ref, sem).wait()

    loads = [
        pltpu.make_async_copy(src, dst, load_sem.at[k])
        for k, (src, dst) in enumerate(
            [
                (res_keys, rk),
                (res_values, rv),
                (pool_keys, pk),
                (pool_values, pv),
                (weight, wv),
                (page_source_in, page_source),
                (page_index_in, page_index),
                (queries_in, queries),
                (new_keys_in, new_keys),
                (new_values_in, new_values),
                (res_len_in, res_len),
                (new_len_in, new_len),
                (partner_bit_in, partner_bit),
                (migrate_out_in, migrate_out),
            ]
        )
    ]
    for k in (5, 6, 7, 11, 10, 8, 9, 12, 13, 0, 1, 2, 3, 4):
        loads[k].start()

    barrier = pltpu.get_barrier_semaphore()
    for zi in range(1, NZ):
        pl.semaphore_signal(barrier, inc=1, device_id=(line(zi), tp), device_id_type=MESH)
    for r in range(1, PEERS):
        pl.semaphore_signal(barrier, inc=1, device_id=(peers[r], tp), device_id_type=MESH)
    for o in range(1, TP):
        pl.semaphore_signal(barrier, inc=1, device_id=(me, tp_peer(o)), device_id_type=MESH)
    loads[5].wait()
    loads[6].wait()
    places = page_source.shape[1]
    count = page_source.shape[0]
    source = page_source[...]
    slot = page_index[...]
    place = iota((count, places), 1)
    lane = iota((count, HD), 1)
    table = jnp.zeros((count, HD), jnp.int32)
    for r in range(PEERS):
        hit = source == peers[r]
        first = jnp.min(jnp.where(hit, place, places), axis=1, keepdims=True)
        last = jnp.max(jnp.where(hit, place, -1), axis=1, keepdims=True)
        last = jnp.where(last > first, last, places)
        for c, p in ((0, first), (1, last)):
            table = jnp.where(lane == 2 * r + c, lax.shift_right_logical(p, NPAGES.bit_length() - 1), table)
            if r == 0:
                page = jnp.max(jnp.where(place == p, slot, 0), axis=1, keepdims=True)
                table = jnp.where(lane == 2 * PEERS + c, page, table)
                skip = (p & (NPAGES - 1)) * PAGE
                table = jnp.where(lane == 2 * PEERS + 2 + c, skip, table)
    tab_v[...] = table
    tab_copy = pltpu.make_async_copy(tab_v, tab, load_sem.at[14])
    tab_copy.start()

    pl.semaphore_wait(barrier, NZ - 1 + PEERS - 1 + TP - 1)

    seq = [0, 1, 7, 2, 6, 3, 5, 4]
    q1_copies = []
    loads[7].wait()
    for i in range(1, NZ):
        zi = seq[i]
        back = seq.index(NZ - zi)
        copy = remote(
            queries.at[pl.ds(RES * ROWS, NEW * ROWS)],
            q1.at[back],
            q1_send.at[i],
            q1_recv.at[back],
            line(zi),
        )
        copy.start()
        q1_copies.append(copy)
    q1[0] = queries[RES * ROWS :, :]

    def forward(i):
        dest = line(order(i))
        block = [q1[i, pl.ds(n * ROWS, ROWS), :] for n in range(NEW)]
        for r in range(PEERS):
            for c in range(2):
                n = tab[dest, 2 * r + c]
                q = lax.select(
                    n == 0,
                    block[0],
                    lax.select(n == 1, block[1], lax.select(n == 2, block[2], block[3])),
                )
                if r == 0:
                    q2[i, 0, pl.ds(c * ROWS, ROWS), :] = q
                else:
                    fw[i, r, pl.ds(c * ROWS, ROWS), :] = q
            if r > 0:
                remote(
                    fw.at[i, r], q2.at[i, mirror(r)], q2_send.at[i], q2_recv.at[i], peers[r]
                ).start()

    tab_copy.wait()
    forward(jnp.int32(0))

    def forward_step(i, carry):
        drain(q1.at[i], q1_recv.at[i])
        forward(i)
        return carry

    lax.fori_loop(1, NZ, forward_step, 0)

    for k in range(8, 14):
        loads[k].wait()
    fresh_count = new_keys.shape[0]
    fresh_k = new_keys[...]
    fresh_v = new_values[...]
    diag = iota((ROWS, HD), 0) == lax.rem(iota((ROWS, HD), 1), ROWS)

    def fresh_scores(request, q):
        s = dot(q, fresh_k, NT) * scale
        row = iota((ROWS, fresh_count), 0)
        col = iota((ROWS, fresh_count), 1)
        live = (lax.div(col, STEPS) == request) & (lax.rem(col, STEPS) <= lax.rem(row, STEPS))
        return jnp.where(live, s, LOW)

    def as_row(column):
        return jnp.sum(jnp.where(diag, column, 0.0), axis=0, keepdims=True)

    quarter = lax.div(iota((1, HD), 1), ROWS)
    for n in range(NEW):
        s = fresh_scores(RES + n, queries[pl.ds((RES + n) * ROWS, ROWS), :])
        m = jnp.max(s, axis=1, keepdims=True)
        p = jnp.exp(s - m)
        l = jnp.sum(p, axis=1, keepdims=True)
        fin[n, 0] = (dot(p.astype(jnp.bfloat16), fresh_v) / l).astype(jnp.bfloat16)
        lf[0, pl.ds(n, 1), :] = as_row(m + jnp.log(l))

    loads[0].wait()
    loads[1].wait()
    context = rk.shape[1]

    def resident_step(i, carry):
        for half in range(2):
            request = 2 * i + half
            q = queries[pl.ds(pl.multiple_of(request * ROWS, ROWS), ROWS), :]
            s = dot(q, rk[request], NT) * scale
            s = jnp.where(iota((ROWS, context), 1) < res_len[me * RES + request], s, LOW)
            f = fresh_scores(request, q)
            m = jnp.maximum(
                jnp.max(s, axis=1, keepdims=True), jnp.max(f, axis=1, keepdims=True)
            )
            p = jnp.exp(s - m)
            g = jnp.exp(f - m)
            l = jnp.sum(p, axis=1, keepdims=True) + jnp.sum(g, axis=1, keepdims=True)
            o = dot(p.astype(jnp.bfloat16), rv[request]) + dot(g.astype(jnp.bfloat16), fresh_v)
            att[pl.ds(pl.multiple_of(request * ROWS, ROWS), ROWS), :] = (o / l).astype(
                jnp.bfloat16
            )
        return carry

    lax.fori_loop(0, RES // 2, resident_step, 0)
    partners = [
        inst_at(x, z, y + 1 - 2 * lax.rem(y, 2)),
        inst_at(x, z, lax.rem(y + 2, NY)),
    ]
    mig_copies = []
    for bit in range(2):
        copy = remote(
            att.at[pl.ds((RES - MIG) * ROWS, MIG * ROWS)],
            guest.at[bit],
            mig_send.at[bit],
            mig_recv.at[bit],
            partners[bit],
        )
        copy.start()
        mig_copies.append(copy)

    loads[2].wait()
    loads[3].wait()
    low_half = lax.rem(lax.div(iota((1, HD), 1), ROWS), 2) == 0
    tile_row = iota((2 * NEW, HD), 0)
    key_lane = iota((ROWS, PAGE), 1)

    def send_part(i, r):
        remote(
            r1s.at[i, r], r1.at[i, mirror(r)], r1_send.at[i], r1_recv.at[i], peers[r]
        ).start()

    def send_level(ip, r):
        remote(
            sts.at[ip, r], st.at[ip, mirror(r)], st_send.at[ip], st_recv.at[ip], peers[r]
        ).start()

    def partial_pair(ip, send, halves=(0, 1)):
        tiles = [jnp.full((2 * NEW, HD), LOW, jnp.float32) for _ in range(PEERS)]
        for half in halves:
            i = 2 * ip + half
            drain(q2.at[i, pl.ds(1, PEERS - 1)], q2_recv.at[i])
            dest_z = lax.rem(z + order(i), NZ)
            for base in range(0, PEERS, 8):
                scores, values, request = [], [], []
                for r in range(base, base + 8):
                    dest = bases[r] + dest_z * NY
                    for c in range(2):
                        n = tab[dest, c]
                        page = tab[dest, 2 * PEERS + c]
                        length = new_len[dest * NEW + jnp.minimum(n, NEW - 1)]
                        live = length - tab[dest, 2 * PEERS + 2 + c]
                        s = dot(q2[i, r, pl.ds(c * ROWS, ROWS), :], pk[page], NT) * scale
                        scores.append(jnp.where(key_lane < live, s, LOW))
                        values.append(pv[page])
                        request.append(n)
                tops = [jnp.max(s, axis=1, keepdims=True) for s in scores]
                exps = [jnp.exp(s - m) for s, m in zip(scores, tops)]
                sums = [jnp.sum(p, axis=1, keepdims=True) for p in exps]
                outs = [
                    (dot(p.astype(jnp.bfloat16), v) / l).astype(jnp.bfloat16)
                    for p, v, l in zip(exps, values, sums)
                ]
                rows = [as_row(m + jnp.log(l)) for m, l in zip(tops, sums)]
                for k, r in enumerate(range(base, base + 8)):
                    for c in range(2):
                        if r == 0:
                            r1[i, 0, pl.ds(c * ROWS, ROWS), :] = outs[2 * k + c]
                        else:
                            r1s[i, r, pl.ds(c * ROWS, ROWS), :] = outs[2 * k + c]
                    level = jnp.where(low_half, rows[2 * k], rows[2 * k + 1])
                    wanted = jnp.where(low_half, request[2 * k], request[2 * k + 1]) + half * NEW
                    filled = jnp.where(low_half, request[2 * k], request[2 * k + 1]) < NEW
                    tiles[r] = jnp.where((tile_row == wanted) & filled, level, tiles[r])
                    if r > 0 and send:
                        send_part(i, r)
        for r in range(PEERS):
            if r == 0:
                st[ip, 0] = tiles[0]
            else:
                sts[ip, r] = tiles[r]
                if send:
                    send_level(ip, r)

    def partial_step(ip, carry):
        partial_pair(ip, True)
        return carry

    lax.fori_loop(1, NZ // 2, partial_step, 0)
    partial_pair(jnp.int32(0), True, (1, 0))

    for copy in mig_copies:
        copy.wait()
    bit = partner_bit[me]
    hand_here = migrate_out[me]
    hand_there = lax.select(bit == 0, migrate_out[partners[0]], migrate_out[partners[1]])
    nothing = jnp.zeros((ROWS, HD), jnp.bfloat16)
    for r in range(RES):
        attm[pl.ds(r * ROWS, ROWS), :] = lax.select(
            r < RES - hand_here, att[pl.ds(r * ROWS, ROWS), :], nothing
        )
    for m in range(MIG):
        came = lax.select(
            bit == 0, guest[0, pl.ds(m * ROWS, ROWS), :], guest[1, pl.ds(m * ROWS, ROWS), :]
        )
        attm[pl.ds((RES + m) * ROWS, ROWS), :] = lax.select(
            m >= MIG - hand_there, came, nothing
        )

    def by_head(values, slots):
        size = slots * ROWS
        row = iota((size, size), 0)
        col = iota((size, size), 1)
        goal = (
            lax.rem(lax.div(row, STEPS), slots) * ROWS
            + lax.div(row, STEPS * slots) * STEPS
            + lax.rem(row, STEPS)
        )
        moved = dot(jnp.where(col == goal, 1.0, 0.0).astype(jnp.bfloat16), values)
        return moved.astype(jnp.bfloat16)

    moved = by_head(attm[...], RES + MIG)
    lead = (RES + MIG) * STEPS
    for h in range(ROWS // STEPS):
        xres[:, pl.ds(h * HD, HD)] = moved[h * lead : (h + 1) * lead]
    loads[4].wait()
    width = out.shape[1]

    def project(rows_ref, sends, send_sem, recv, recv_sem, own):
        copies = []
        for o in (3, 2, 1, 0):
            peer = tp_peer(o)
            part = dot(rows_ref[...], wv[:, pl.ds(pl.multiple_of(peer * width, width), width)])
            if o == 0:
                own[...] = part
            else:
                sends[o] = part.astype(jnp.bfloat16)
                copy = remote(sends.at[o], recv.at[o], send_sem.at[o], recv_sem.at[o], me, peer)
                copy.start()
                copies.append(copy)
        return copies

    rs1_copies = project(xres, rs1s, rs1_send, rs1, rs1_recv, own1)

    low = iota((2 * NEW, HD), 1) < 2 * ROWS

    def pair_levels(ip):
        drain(st.at[ip, pl.ds(1, PEERS - 1)], st_recv.at[ip])
        return [
            jnp.where(low, st[ip, 2 * q], st[ip, 2 * q + 1]) for q in range(PEERS // 2)
        ]

    def softmax_over(levels):
        m = levels[0]
        for level in levels[1:]:
            m = jnp.maximum(m, level)
        m = jnp.maximum(m, pltpu.roll(m, 2 * ROWS, 1))
        m = jnp.maximum(m, pltpu.roll(m, ROWS, 1))
        shares = [jnp.exp(level - m) for level in levels]
        total = shares[0]
        for share in shares[1:]:
            total = total + share
        total = total + pltpu.roll(total, 2 * ROWS, 1)
        total = total + pltpu.roll(total, ROWS, 1)
        return [share / total for share in shares], m + jnp.log(total)

    def merge(ip, levels, halves):
        shares, together = softmax_over(levels)
        ls[ip] = together
        for half in halves:
            i = 2 * ip + half
            drain(r1.at[i, pl.ds(1, PEERS - 1)], r1_recv.at[i])
            blocks = []
            for n in range(NEW):
                k = half * NEW + n
                blocks.append(
                    jnp.concatenate(
                        [jnp.where(diag, share[k : k + 1], 0.0) for share in shares], axis=1
                    )
                )
            mix = jnp.concatenate(blocks, axis=0).astype(jnp.bfloat16)
            merged = dot(mix, r1[i].reshape(PEERS * 2 * ROWS, HD)).astype(jnp.bfloat16)
            for n in range(NEW):
                r2s[i, n] = merged[n * ROWS : (n + 1) * ROWS]
            zi = order(i)
            turned = i + 1 - 2 * lax.rem(i + 1, 2)
            back = turned - lax.div(turned, NZ)
            remote(
                r2s.at[i], fin.at[:, back], r2_send.at[i], r2_recv.at[back], line(zi)
            ).start()
            remote(ls.at[ip], lf.at[back], lf_send.at[i], lf_recv.at[back], line(zi)).start()

    def merge_step(ip, carry):
        merge(ip, pair_levels(ip), (0, 1))
        return carry

    lax.fori_loop(1, NZ // 2, merge_step, 0)
    near = pair_levels(0)
    merge(jnp.int32(0), near, (1,))

    drain(r1.at[0, pl.ds(1, PEERS - 1)], r1_recv.at[0])
    for i in range(1, NZ):
        drain(lf.at[i], lf_recv.at[i])
        drain(fin.at[:, i], r2_recv.at[i])
    from_odd = [False, False, True, False, True, False, True, True]
    levels = [level[:NEW] for level in near]
    for base in range(0, NZ, 4):
        level = jnp.full((NEW, HD), LOW, jnp.float32)
        for g in range(4):
            i = base + g
            rows = lf[i, pl.ds(NEW if from_odd[i] else 0, NEW), :]
            level = jnp.where(quarter == g, rows, level)
        levels.append(level)
    shares, _ = softmax_over(levels)
    tail = NEW * STEPS
    row = iota((tail, HD), 0)
    spread = []
    for share in shares:
        wide = jnp.zeros((tail, HD), jnp.float32)
        for n in range(NEW):
            wide = jnp.where(lax.div(row, STEPS) == n, share[n : n + 1], wide)
        spread.append(wide)
    column = lax.rem(iota((tail, HD), 1), ROWS) - lax.rem(row, STEPS)
    owner = lax.div(row, STEPS)

    def mixing(parts, n):
        rows = []
        for h in range(ROWS // STEPS):
            keep = column == h * STEPS
            if n is not None:
                keep = keep & (owner == n)
            rows.append(
                jnp.concatenate([jnp.where(keep, part, 0.0) for part in parts], axis=1)
            )
        return jnp.concatenate(rows, axis=0).astype(jnp.bfloat16)

    attended = dot(mixing(spread[: PEERS // 2], None), r1[0].reshape(PEERS * 2 * ROWS, HD))
    for n in range(NEW):
        attended = attended + dot(
            mixing(spread[PEERS // 2 :], n), fin[n].reshape(NZ * ROWS, HD)
        )
    attended = attended.astype(jnp.bfloat16)
    for h in range(ROWS // STEPS):
        xnew[:, pl.ds(h * HD, HD)] = attended[h * tail : (h + 1) * tail]
    rs2_copies = project(xnew, rs2s, rs2_send, rs2, rs2_recv, own2)

    for copy in rs1_copies:
        copy.wait()
    total = own1[...]
    for o in range(1, TP):
        total = total + rs1[o].astype(jnp.float32)
    out[pl.ds(0, lead), :] = total.astype(jnp.bfloat16)
    for copy in q1_copies:
        copy.wait_send()
    for i in range(NZ):
        drain(fw.at[i, pl.ds(1, PEERS - 1)], q2_send.at[i])
        drain(r1s.at[i, pl.ds(1, PEERS - 1)], r1_send.at[i])
        if i > 0:
            drain(r2s.at[i], r2_send.at[i])
            drain(ls.at[i // 2], lf_send.at[i])
    for ip in range(NZ // 2):
        drain(sts.at[ip, pl.ds(1, PEERS - 1)], st_send.at[ip])
    for copy in rs2_copies:
        copy.wait()
    total = own2[...]
    for o in range(1, TP):
        total = total + rs2[o].astype(jnp.float32)
    out[pl.ds(lead, tail), :] = total.astype(jnp.bfloat16)


def per_device(
    res_keys,
    res_values,
    pool_keys,
    pool_values,
    queries,
    new_keys,
    new_values,
    res_len,
    new_len,
    page_source,
    page_index,
    partner_bit,
    migrate_out,
    out_weight,
):
    bf, f32 = jnp.bfloat16, jnp.float32
    rows = (RES + MIG + NEW) * STEPS
    lead, tail = (RES + MIG) * STEPS, NEW * STEPS
    width = out_weight.shape[1] // TP
    vmem = pl.BlockSpec(memory_space=pltpu.VMEM)
    hbm = pl.BlockSpec(memory_space=pltpu.HBM)
    dma = pltpu.SemaphoreType.DMA
    depth = out_weight.shape[0]
    whole = [
        pltpu.SMEM(res_len.shape, jnp.int32),
        pltpu.SMEM(new_len.shape, jnp.int32),
        pltpu.SMEM(partner_bit.shape, jnp.int32),
        pltpu.SMEM(migrate_out.shape, jnp.int32),
        pltpu.VMEM(page_source.shape, jnp.int32),
        pltpu.VMEM(page_index.shape, jnp.int32),
        pltpu.VMEM((queries.shape[0] * ROWS, HD), bf),
        pltpu.VMEM((queries.shape[0] * STEPS, HD), bf),
        pltpu.VMEM((queries.shape[0] * STEPS, HD), bf),
    ]
    scratch = whole + [
        pltpu.VMEM((RES, res_keys.shape[2], HD), bf),
        pltpu.VMEM((RES, res_keys.shape[2], HD), bf),
        pltpu.VMEM((pool_keys.shape[0], PAGE, HD), bf),
        pltpu.VMEM((pool_keys.shape[0], PAGE, HD), bf),
        pltpu.VMEM(out_weight.shape, bf),
        pltpu.VMEM((page_source.shape[0], HD), jnp.int32),
        pltpu.SMEM((page_source.shape[0], HD), jnp.int32),
        pltpu.VMEM((NZ, NEW * ROWS, HD), bf),
        pltpu.VMEM((NZ, PEERS, 2 * ROWS, HD), bf),
        pltpu.VMEM((NZ, PEERS, 2 * ROWS, HD), bf),
        pltpu.VMEM((NZ, PEERS, 2 * ROWS, HD), bf),
        pltpu.VMEM((NZ, PEERS, 2 * ROWS, HD), bf),
        pltpu.VMEM((NZ // 2, PEERS, 2 * NEW, HD), f32),
        pltpu.VMEM((NZ // 2, PEERS, 2 * NEW, HD), f32),
        pltpu.VMEM((NZ, NEW, ROWS, HD), bf),
        pltpu.VMEM((NZ // 2, 2 * NEW, HD), f32),
        pltpu.VMEM((NEW, NZ, ROWS, HD), bf),
        pltpu.VMEM((NZ, 2 * NEW, HD), f32),
        pltpu.VMEM((RES * ROWS, HD), bf),
        pltpu.VMEM((2, MIG * ROWS, HD), bf),
        pltpu.VMEM(((RES + MIG) * ROWS, HD), bf),
        pltpu.VMEM((lead, depth), bf),
        pltpu.VMEM((tail, depth), bf),
        pltpu.VMEM((lead, width), f32),
        pltpu.VMEM((tail, width), f32),
        pltpu.VMEM((TP, lead, width), bf),
        pltpu.VMEM((TP, lead, width), bf),
        pltpu.VMEM((TP, tail, width), bf),
        pltpu.VMEM((TP, tail, width), bf),
        dma((15,)),
        dma((NZ,)),
        dma((NZ,)),
        dma((NZ,)),
        dma((NZ,)),
        dma((NZ,)),
        dma((NZ,)),
        dma((NZ // 2,)),
        dma((NZ // 2,)),
        dma((NZ,)),
        dma((NZ,)),
        dma((NZ,)),
        dma((NZ,)),
        dma((2,)),
        dma((2,)),
        dma((TP,)),
        dma((TP,)),
        dma((TP,)),
        dma((TP,)),
    ]
    return pl.pallas_call(
        kernel,
        out_shape=jax.ShapeDtypeStruct((rows, width), bf),
        in_specs=[hbm] * 14,
        out_specs=vmem,
        scratch_shapes=scratch,
        compiler_params=pltpu.CompilerParams(
            collective_id=0, has_side_effects=True, vmem_limit_bytes=48 * 2**20
        ),
        cost_estimate=pl.CostEstimate(
            flops=10**9, bytes_accessed=16 * 2**20, transcendentals=10**6
        ),
    )(
        *(
            pltpu.with_memory_space_constraint(operand, pltpu.HBM)
            for operand in (
                res_len,
                new_len,
                partner_bit,
                migrate_out,
                page_source,
                page_index,
                queries.reshape(-1, HD),
                new_keys.reshape(-1, HD),
                new_values.reshape(-1, HD),
                res_keys.reshape(RES, -1, HD),
                res_values.reshape(RES, -1, HD),
                pool_keys.reshape(-1, PAGE, HD),
                pool_values.reshape(-1, PAGE, HD),
                out_weight,
            )
        )
    )


def solution(mesh):
    heads = P("inst", "tp", None, None)
    in_specs = (heads,) * 7 + (P(),) * 6 + (P("tp", None),)
    return jax.shard_map(
        per_device, mesh=mesh, in_specs=in_specs, out_specs=P("inst", "tp"), check_vma=False
    )
```

```python
import math

import jax
import jax.numpy as jnp
from jax import lax
from jax.experimental import pallas as pl
from jax.experimental.pallas import tpu as pltpu
from jax.sharding import PartitionSpec as P

MESH = pl.DeviceIdType.MESH
NX, NZ, NY = 2, 8, 4
PEERS = NX * NY
TP = 4
RES, NEW, MIG = 6, 4, 2
STEPS = 4
ROWS = 32
HD = 128
PAGE = 128
NPAGES = 16
LOW = -1e30
NT = (((1,), (1,)), ((), ()))
NN = (((1,), (0,)), ((), ()))


def mirror(r):
    dx, dy = divmod(r, NY)
    return dx * NY + (NY - dy) % NY


def iota(shape, axis):
    return lax.broadcasted_iota(jnp.int32, shape, axis)


def dot(a, b, dims=NN):
    return lax.dot_general(a, b, dims, preferred_element_type=jnp.float32)


def kernel(
    res_len_in,
    new_len_in,
    partner_bit_in,
    migrate_out_in,
    page_source_in,
    page_index_in,
    queries_in,
    new_keys_in,
    new_values_in,
    res_keys,
    res_values,
    pool_keys,
    pool_values,
    weight,
    out,
    res_len,
    new_len,
    partner_bit,
    migrate_out,
    page_source,
    page_index,
    queries,
    new_keys,
    new_values,
    rk,
    rv,
    pk,
    pv,
    wv,
    tab_v,
    tab,
    q1,
    fw,
    q2,
    r1s,
    r1,
    sts,
    st,
    r2s,
    ls,
    fin,
    lf,
    att,
    guest,
    attm,
    xres,
    xnew,
    own1,
    own2,
    rs1s,
    rs1,
    rs2s,
    rs2,
    load_sem,
    q1_send,
    q1_recv,
    q2_send,
    q2_recv,
    r1_send,
    r1_recv,
    st_send,
    st_recv,
    r2_send,
    r2_recv,
    lf_send,
    lf_recv,
    mig_send,
    mig_recv,
    rs1_send,
    rs1_recv,
    rs2_send,
    rs2_recv,
):
    me = lax.axis_index("inst")
    tp = lax.axis_index("tp")
    y = lax.rem(me, NY)
    z = lax.rem(lax.div(me, NY), NZ)
    x = lax.div(me, NY * NZ)
    hi = lax.div(tp, 2)
    core = lax.rem(tp, 2)
    scale = 1.0 / math.sqrt(HD)

    def inst_at(xx, zz, yy):
        return (xx * NZ + zz) * NY + yy

    def plane(r, zz):
        dx, dy = divmod(r, NY)
        return inst_at(lax.rem(x + dx, NX), zz, lax.rem(y + dy, NY))

    def line(zi):
        return inst_at(x, lax.rem(z + zi, NZ), y)

    bases = [plane(r, 0) for r in range(PEERS)]
    peers = [base + z * NY for base in bases]

    def tp_peer(o):
        return lax.rem(hi + o // 2, 2) * 2 + lax.rem(core + o % 2, 2)

    def order(i):
        odd = lax.rem(i, 2)
        return lax.rem(odd * lax.div(i + 1, 2) + (1 - odd) * (NZ - lax.div(i, 2)), NZ)

    def remote(src, dst, send, recv, inst, t=tp):
        return pltpu.make_async_remote_copy(
            src_ref=src,
            dst_ref=dst,
            send_sem=send,
            recv_sem=recv,
            device_id=(inst, t),
            device_id_type=MESH,
        )

    def drain(ref, sem):
        pltpu.make_async_copy(ref, ref, sem).wait()

    loads = [
        pltpu.make_async_copy(src, dst, load_sem.at[k])
        for k, (src, dst) in enumerate(
            [
                (res_keys, rk),
                (res_values, rv),
                (pool_keys, pk),
                (pool_values, pv),
                (weight, wv),
                (page_source_in, page_source),
                (page_index_in, page_index),
                (queries_in, queries),
                (new_keys_in, new_keys),
                (new_values_in, new_values),
                (res_len_in, res_len),
                (new_len_in, new_len),
                (partner_bit_in, partner_bit),
                (migrate_out_in, migrate_out),
            ]
        )
    ]
    for k in (5, 6, 7, 11, 10, 8, 9, 12, 13, 0, 1, 2, 3, 4):
        loads[k].start()

    barrier = pltpu.get_barrier_semaphore()
    for zi in range(1, NZ):
        pl.semaphore_signal(barrier, inc=1, device_id=(line(zi), tp), device_id_type=MESH)
    for r in range(1, PEERS):
        pl.semaphore_signal(barrier, inc=1, device_id=(peers[r], tp), device_id_type=MESH)
    for o in range(1, TP):
        pl.semaphore_signal(barrier, inc=1, device_id=(me, tp_peer(o)), device_id_type=MESH)
    loads[5].wait()
    loads[6].wait()
    places = page_source.shape[1]
    count = page_source.shape[0]
    source = page_source[...]
    slot = page_index[...]
    place = iota((count, places), 1)
    lane = iota((count, HD), 1)
    table = jnp.zeros((count, HD), jnp.int32)
    for r in range(PEERS):
        hit = source == peers[r]
        first = jnp.min(jnp.where(hit, place, places), axis=1, keepdims=True)
        last = jnp.max(jnp.where(hit, place, -1), axis=1, keepdims=True)
        last = jnp.where(last > first, last, places)
        for c, p in ((0, first), (1, last)):
            table = jnp.where(lane == 2 * r + c, lax.shift_right_logical(p, NPAGES.bit_length() - 1), table)
            if r == 0:
                page = jnp.max(jnp.where(place == p, slot, 0), axis=1, keepdims=True)
                table = jnp.where(lane == 2 * PEERS + c, page, table)
                skip = (p & (NPAGES - 1)) * PAGE
                table = jnp.where(lane == 2 * PEERS + 2 + c, skip, table)
    tab_v[...] = table
    tab_copy = pltpu.make_async_copy(tab_v, tab, load_sem.at[14])
    tab_copy.start()

    pl.semaphore_wait(barrier, NZ - 1 + PEERS - 1 + TP - 1)

    seq = [0, 1, 7, 2, 6, 3, 5, 4]
    q1_copies = []
    loads[7].wait()
    for i in range(1, NZ):
        zi = seq[i]
        back = seq.index(NZ - zi)
        copy = remote(
            queries.at[pl.ds(RES * ROWS, NEW * ROWS)],
            q1.at[back],
            q1_send.at[i],
            q1_recv.at[back],
            line(zi),
        )
        copy.start()
        q1_copies.append(copy)
    q1[0] = queries[RES * ROWS :, :]

    def forward(i):
        dest = line(order(i))
        block = [q1[i, pl.ds(n * ROWS, ROWS), :] for n in range(NEW)]
        for r in range(PEERS):
            for c in range(2):
                n = tab[dest, 2 * r + c]
                q = lax.select(
                    n == 0,
                    block[0],
                    lax.select(n == 1, block[1], lax.select(n == 2, block[2], block[3])),
                )
                if r == 0:
                    q2[i, 0, pl.ds(c * ROWS, ROWS), :] = q
                else:
                    fw[i, r, pl.ds(c * ROWS, ROWS), :] = q
            if r > 0:
                remote(
                    fw.at[i, r], q2.at[i, mirror(r)], q2_send.at[i], q2_recv.at[i], peers[r]
                ).start()

    tab_copy.wait()
    forward(jnp.int32(0))

    def forward_step(i, carry):
        drain(q1.at[i], q1_recv.at[i])
        forward(i)
        return carry

    lax.fori_loop(1, NZ, forward_step, 0)

    for k in range(8, 14):
        loads[k].wait()
    fresh_count = new_keys.shape[0]
    fresh_k = new_keys[...]
    fresh_v = new_values[...]
    diag = iota((ROWS, HD), 0) == lax.rem(iota((ROWS, HD), 1), ROWS)

    def fresh_scores(request, q):
        s = dot(q, fresh_k, NT) * scale
        row = iota((ROWS, fresh_count), 0)
        col = iota((ROWS, fresh_count), 1)
        live = (lax.div(col, STEPS) == request) & (lax.rem(col, STEPS) <= lax.rem(row, STEPS))
        return jnp.where(live, s, LOW)

    def as_row(column):
        return jnp.sum(jnp.where(diag, column, 0.0), axis=0, keepdims=True)

    quarter = lax.div(iota((1, HD), 1), ROWS)
    for n in range(NEW):
        s = fresh_scores(RES + n, queries[pl.ds((RES + n) * ROWS, ROWS), :])
        m = jnp.max(s, axis=1, keepdims=True)
        p = jnp.exp(s - m)
        l = jnp.sum(p, axis=1, keepdims=True)
        fin[n, 0] = (dot(p.astype(jnp.bfloat16), fresh_v) / l).astype(jnp.bfloat16)
        lf[0, pl.ds(n, 1), :] = as_row(m + jnp.log(l))

    loads[0].wait()
    loads[1].wait()
    context = rk.shape[1]

    def resident_step(i, carry):
        for half in range(2):
            request = 2 * i + half
            q = queries[pl.ds(pl.multiple_of(request * ROWS, ROWS), ROWS), :]
            s = dot(q, rk[request], NT) * scale
            s = jnp.where(iota((ROWS, context), 1) < res_len[me * RES + request], s, LOW)
            f = fresh_scores(request, q)
            m = jnp.maximum(
                jnp.max(s, axis=1, keepdims=True), jnp.max(f, axis=1, keepdims=True)
            )
            p = jnp.exp(s - m)
            g = jnp.exp(f - m)
            l = jnp.sum(p, axis=1, keepdims=True) + jnp.sum(g, axis=1, keepdims=True)
            o = dot(p.astype(jnp.bfloat16), rv[request]) + dot(g.astype(jnp.bfloat16), fresh_v)
            att[pl.ds(pl.multiple_of(request * ROWS, ROWS), ROWS), :] = (o / l).astype(
                jnp.bfloat16
            )
        return carry

    lax.fori_loop(0, RES // 2, resident_step, 0)
    partners = [
        inst_at(x, z, y + 1 - 2 * lax.rem(y, 2)),
        inst_at(x, z, lax.rem(y + 2, NY)),
    ]
    mig_copies = []
    for bit in range(2):
        copy = remote(
            att.at[pl.ds((RES - MIG) * ROWS, MIG * ROWS)],
            guest.at[bit],
            mig_send.at[bit],
            mig_recv.at[bit],
            partners[bit],
        )
        copy.start()
        mig_copies.append(copy)

    loads[2].wait()
    loads[3].wait()
    low_half = lax.rem(lax.div(iota((1, HD), 1), ROWS), 2) == 0
    tile_row = iota((2 * NEW, HD), 0)
    key_lane = iota((ROWS, PAGE), 1)

    def send_part(i, r):
        remote(
            r1s.at[i, r], r1.at[i, mirror(r)], r1_send.at[i], r1_recv.at[i], peers[r]
        ).start()

    def send_level(tile):
        for r in range(1, PEERS):
            remote(
                sts.at[tile, r],
                st.at[tile, mirror(r)],
                st_send.at[tile],
                st_recv.at[tile],
                peers[r],
            ).start()

    tile_of = {1: (0, 0), 2: (0, 1), 3: (1, 0), 0: (1, 1)}
    low = iota((2 * NEW, HD), 1) < 2 * ROWS

    def partial_pair(ip, halves=(0, 1)):
        tiles = [jnp.full((2 * NEW, HD), LOW, jnp.float32) for _ in range(PEERS)]
        for half in halves:
            i = jnp.int32(2 * ip + half)
            drain(q2.at[i, pl.ds(1, PEERS - 1)], q2_recv.at[i])
            dest_z = lax.rem(z + order(i), NZ)
            for base in range(0, PEERS, 8):
                scores, values, request = [], [], []
                for r in range(base, base + 8):
                    dest = bases[r] + dest_z * NY
                    for c in range(2):
                        n = tab[dest, c]
                        page = tab[dest, 2 * PEERS + c]
                        length = new_len[dest * NEW + jnp.minimum(n, NEW - 1)]
                        live = length - tab[dest, 2 * PEERS + 2 + c]
                        s = dot(q2[i, r, pl.ds(c * ROWS, ROWS), :], pk[page], NT) * scale
                        scores.append(jnp.where(key_lane < live, s, LOW))
                        values.append(pv[page])
                        request.append(n)
                tops = [jnp.max(s, axis=1, keepdims=True) for s in scores]
                exps = [jnp.exp(s - m) for s, m in zip(scores, tops)]
                sums = [jnp.sum(p, axis=1, keepdims=True) for p in exps]
                outs = [
                    (dot(p.astype(jnp.bfloat16), v) / l).astype(jnp.bfloat16)
                    for p, v, l in zip(exps, values, sums)
                ]
                rows = [as_row(m + jnp.log(l)) for m, l in zip(tops, sums)]
                for k, r in enumerate(range(base, base + 8)):
                    for c in range(2):
                        if r == 0:
                            r1[i, 0, pl.ds(c * ROWS, ROWS), :] = outs[2 * k + c]
                        else:
                            r1s[i, r, pl.ds(c * ROWS, ROWS), :] = outs[2 * k + c]
                    level = jnp.where(low_half, rows[2 * k], rows[2 * k + 1])
                    wanted = jnp.where(low_half, request[2 * k], request[2 * k + 1]) + half * NEW
                    filled = jnp.where(low_half, request[2 * k], request[2 * k + 1]) < NEW
                    tiles[r] = jnp.where((tile_row == wanted) & filled, level, tiles[r])
                    if r > 0:
                        send_part(i, r)
        tile, second = tile_of[ip]
        for r in range(PEERS):
            into = sts if r > 0 else st
            if second:
                into[tile, r] = jnp.where(low, into[tile, r], tiles[r])
            else:
                into[tile, r] = tiles[r]
        if second:
            send_level(tile)

    for ip in (1, 2, 3):
        partial_pair(ip)
    partial_pair(0, (1, 0))

    for copy in mig_copies:
        copy.wait()
    bit = partner_bit[me]
    hand_here = migrate_out[me]
    hand_there = lax.select(bit == 0, migrate_out[partners[0]], migrate_out[partners[1]])
    nothing = jnp.zeros((ROWS, HD), jnp.bfloat16)
    for r in range(RES):
        attm[pl.ds(r * ROWS, ROWS), :] = lax.select(
            r < RES - hand_here, att[pl.ds(r * ROWS, ROWS), :], nothing
        )
    for m in range(MIG):
        came = lax.select(
            bit == 0, guest[0, pl.ds(m * ROWS, ROWS), :], guest[1, pl.ds(m * ROWS, ROWS), :]
        )
        attm[pl.ds((RES + m) * ROWS, ROWS), :] = lax.select(
            m >= MIG - hand_there, came, nothing
        )

    def by_head(values, slots):
        size = slots * ROWS
        row = iota((size, size), 0)
        col = iota((size, size), 1)
        goal = (
            lax.rem(lax.div(row, STEPS), slots) * ROWS
            + lax.div(row, STEPS * slots) * STEPS
            + lax.rem(row, STEPS)
        )
        moved = dot(jnp.where(col == goal, 1.0, 0.0).astype(jnp.bfloat16), values)
        return moved.astype(jnp.bfloat16)

    moved = by_head(attm[...], RES + MIG)
    lead = (RES + MIG) * STEPS
    for h in range(ROWS // STEPS):
        xres[:, pl.ds(h * HD, HD)] = moved[h * lead : (h + 1) * lead]
    loads[4].wait()
    width = out.shape[1]

    def project(rows_ref, sends, send_sem, recv, recv_sem, own):
        copies = []
        for o in (3, 2, 1, 0):
            peer = tp_peer(o)
            part = dot(rows_ref[...], wv[:, pl.ds(pl.multiple_of(peer * width, width), width)])
            if o == 0:
                own[...] = part
            else:
                sends[o] = part.astype(jnp.bfloat16)
                copy = remote(sends.at[o], recv.at[o], send_sem.at[o], recv_sem.at[o], me, peer)
                copy.start()
                copies.append(copy)
        return copies

    rs1_copies = project(xres, rs1s, rs1_send, rs1, rs1_recv, own1)

    def pair_levels(ip):
        tile, second = tile_of[ip]
        levels = []
        for q in range(0, PEERS, 2):
            left, right = st[tile, q], st[tile, q + 1]
            if second:
                left = pltpu.roll(left, 2 * ROWS, 1)
            else:
                right = pltpu.roll(right, 2 * ROWS, 1)
            levels.append(jnp.where(low, left, right))
        return levels

    def softmax_over(levels):
        m = levels[0]
        for level in levels[1:]:
            m = jnp.maximum(m, level)
        m = jnp.maximum(m, pltpu.roll(m, 2 * ROWS, 1))
        m = jnp.maximum(m, pltpu.roll(m, ROWS, 1))
        shares = [jnp.exp(level - m) for level in levels]
        total = shares[0]
        for share in shares[1:]:
            total = total + share
        total = total + pltpu.roll(total, 2 * ROWS, 1)
        total = total + pltpu.roll(total, ROWS, 1)
        return [share / total for share in shares], m + jnp.log(total)

    def merge(ip, levels, halves):
        shares, together = softmax_over(levels)
        ls[ip] = together
        for half in halves:
            i = 2 * ip + half
            drain(r1.at[i, pl.ds(1, PEERS - 1)], r1_recv.at[i])
            blocks = []
            for n in range(NEW):
                k = half * NEW + n
                blocks.append(
                    jnp.concatenate(
                        [jnp.where(diag, share[k : k + 1], 0.0) for share in shares], axis=1
                    )
                )
            mix = jnp.concatenate(blocks, axis=0).astype(jnp.bfloat16)
            merged = dot(mix, r1[i].reshape(PEERS * 2 * ROWS, HD)).astype(jnp.bfloat16)
            for n in range(NEW):
                r2s[i, n] = merged[n * ROWS : (n + 1) * ROWS]
            zi = order(i)
            turned = i + 1 - 2 * lax.rem(i + 1, 2)
            back = turned - lax.div(turned, NZ)
            remote(
                r2s.at[i], fin.at[:, back], r2_send.at[i], r2_recv.at[back], line(zi)
            ).start()
            remote(ls.at[ip], lf.at[back], lf_send.at[i], lf_recv.at[back], line(zi)).start()

    for ip in (1, 2, 3):
        if ip != 2:
            tile = tile_of[ip][0]
            drain(st.at[tile, pl.ds(1, PEERS - 1)], st_recv.at[tile])
        merge(jnp.int32(ip), pair_levels(ip), (0, 1))
    near = pair_levels(0)
    merge(jnp.int32(0), near, (1,))

    drain(r1.at[0, pl.ds(1, PEERS - 1)], r1_recv.at[0])
    for i in range(1, NZ):
        drain(lf.at[i], lf_recv.at[i])
        drain(fin.at[:, i], r2_recv.at[i])
    from_odd = [False, False, True, False, True, False, True, True]
    levels = [level[:NEW] for level in near]
    for base in range(0, NZ, 4):
        level = jnp.full((NEW, HD), LOW, jnp.float32)
        for g in range(4):
            i = base + g
            rows = lf[i, pl.ds(NEW if from_odd[i] else 0, NEW), :]
            level = jnp.where(quarter == g, rows, level)
        levels.append(level)
    shares, _ = softmax_over(levels)
    tail = NEW * STEPS
    row = iota((tail, HD), 0)
    spread = []
    for share in shares:
        wide = jnp.zeros((tail, HD), jnp.float32)
        for n in range(NEW):
            wide = jnp.where(lax.div(row, STEPS) == n, share[n : n + 1], wide)
        spread.append(wide)
    column = lax.rem(iota((tail, HD), 1), ROWS) - lax.rem(row, STEPS)
    owner = lax.div(row, STEPS)

    def mixing(parts, n):
        rows = []
        for h in range(ROWS // STEPS):
            keep = column == h * STEPS
            if n is not None:
                keep = keep & (owner == n)
            rows.append(
                jnp.concatenate([jnp.where(keep, part, 0.0) for part in parts], axis=1)
            )
        return jnp.concatenate(rows, axis=0).astype(jnp.bfloat16)

    attended = dot(mixing(spread[: PEERS // 2], None), r1[0].reshape(PEERS * 2 * ROWS, HD))
    for n in range(NEW):
        attended = attended + dot(
            mixing(spread[PEERS // 2 :], n), fin[n].reshape(NZ * ROWS, HD)
        )
    attended = attended.astype(jnp.bfloat16)
    for h in range(ROWS // STEPS):
        xnew[:, pl.ds(h * HD, HD)] = attended[h * tail : (h + 1) * tail]
    rs2_copies = project(xnew, rs2s, rs2_send, rs2, rs2_recv, own2)

    for copy in rs1_copies:
        copy.wait()
    total = own1[...]
    for o in range(1, TP):
        total = total + rs1[o].astype(jnp.float32)
    out[pl.ds(0, lead), :] = total.astype(jnp.bfloat16)
    for copy in q1_copies:
        copy.wait_send()
    for i in range(NZ):
        drain(fw.at[i, pl.ds(1, PEERS - 1)], q2_send.at[i])
        drain(r1s.at[i, pl.ds(1, PEERS - 1)], r1_send.at[i])
        if i > 0:
            drain(r2s.at[i], r2_send.at[i])
            drain(ls.at[i // 2], lf_send.at[i])
    for tile in range(2):
        drain(sts.at[tile, pl.ds(1, PEERS - 1)], st_send.at[tile])
    for copy in rs2_copies:
        copy.wait()
    total = own2[...]
    for o in range(1, TP):
        total = total + rs2[o].astype(jnp.float32)
    out[pl.ds(lead, tail), :] = total.astype(jnp.bfloat16)


def per_device(
    res_keys,
    res_values,
    pool_keys,
    pool_values,
    queries,
    new_keys,
    new_values,
    res_len,
    new_len,
    page_source,
    page_index,
    partner_bit,
    migrate_out,
    out_weight,
):
    bf, f32 = jnp.bfloat16, jnp.float32
    rows = (RES + MIG + NEW) * STEPS
    lead, tail = (RES + MIG) * STEPS, NEW * STEPS
    width = out_weight.shape[1] // TP
    vmem = pl.BlockSpec(memory_space=pltpu.VMEM)
    hbm = pl.BlockSpec(memory_space=pltpu.HBM)
    dma = pltpu.SemaphoreType.DMA
    depth = out_weight.shape[0]
    whole = [
        pltpu.SMEM(res_len.shape, jnp.int32),
        pltpu.SMEM(new_len.shape, jnp.int32),
        pltpu.SMEM(partner_bit.shape, jnp.int32),
        pltpu.SMEM(migrate_out.shape, jnp.int32),
        pltpu.VMEM(page_source.shape, jnp.int32),
        pltpu.VMEM(page_index.shape, jnp.int32),
        pltpu.VMEM((queries.shape[0] * ROWS, HD), bf),
        pltpu.VMEM((queries.shape[0] * STEPS, HD), bf),
        pltpu.VMEM((queries.shape[0] * STEPS, HD), bf),
    ]
    scratch = whole + [
        pltpu.VMEM((RES, res_keys.shape[2], HD), bf),
        pltpu.VMEM((RES, res_keys.shape[2], HD), bf),
        pltpu.VMEM((pool_keys.shape[0], PAGE, HD), bf),
        pltpu.VMEM((pool_keys.shape[0], PAGE, HD), bf),
        pltpu.VMEM(out_weight.shape, bf),
        pltpu.VMEM((page_source.shape[0], HD), jnp.int32),
        pltpu.SMEM((page_source.shape[0], HD), jnp.int32),
        pltpu.VMEM((NZ, NEW * ROWS, HD), bf),
        pltpu.VMEM((NZ, PEERS, 2 * ROWS, HD), bf),
        pltpu.VMEM((NZ, PEERS, 2 * ROWS, HD), bf),
        pltpu.VMEM((NZ, PEERS, 2 * ROWS, HD), bf),
        pltpu.VMEM((NZ, PEERS, 2 * ROWS, HD), bf),
        pltpu.VMEM((2, PEERS, 2 * NEW, HD), f32),
        pltpu.VMEM((2, PEERS, 2 * NEW, HD), f32),
        pltpu.VMEM((NZ, NEW, ROWS, HD), bf),
        pltpu.VMEM((NZ // 2, 2 * NEW, HD), f32),
        pltpu.VMEM((NEW, NZ, ROWS, HD), bf),
        pltpu.VMEM((NZ, 2 * NEW, HD), f32),
        pltpu.VMEM((RES * ROWS, HD), bf),
        pltpu.VMEM((2, MIG * ROWS, HD), bf),
        pltpu.VMEM(((RES + MIG) * ROWS, HD), bf),
        pltpu.VMEM((lead, depth), bf),
        pltpu.VMEM((tail, depth), bf),
        pltpu.VMEM((lead, width), f32),
        pltpu.VMEM((tail, width), f32),
        pltpu.VMEM((TP, lead, width), bf),
        pltpu.VMEM((TP, lead, width), bf),
        pltpu.VMEM((TP, tail, width), bf),
        pltpu.VMEM((TP, tail, width), bf),
        dma((15,)),
        dma((NZ,)),
        dma((NZ,)),
        dma((NZ,)),
        dma((NZ,)),
        dma((NZ,)),
        dma((NZ,)),
        dma((NZ // 2,)),
        dma((NZ // 2,)),
        dma((NZ,)),
        dma((NZ,)),
        dma((NZ,)),
        dma((NZ,)),
        dma((2,)),
        dma((2,)),
        dma((TP,)),
        dma((TP,)),
        dma((TP,)),
        dma((TP,)),
    ]
    return pl.pallas_call(
        kernel,
        out_shape=jax.ShapeDtypeStruct((rows, width), bf),
        in_specs=[hbm] * 14,
        out_specs=vmem,
        scratch_shapes=scratch,
        compiler_params=pltpu.CompilerParams(
            collective_id=0, has_side_effects=True, vmem_limit_bytes=48 * 2**20
        ),
        cost_estimate=pl.CostEstimate(
            flops=10**9, bytes_accessed=16 * 2**20, transcendentals=10**6
        ),
    )(
        *(
            pltpu.with_memory_space_constraint(operand, pltpu.HBM)
            for operand in (
                res_len,
                new_len,
                partner_bit,
                migrate_out,
                page_source,
                page_index,
                queries.reshape(-1, HD),
                new_keys.reshape(-1, HD),
                new_values.reshape(-1, HD),
                res_keys.reshape(RES, -1, HD),
                res_values.reshape(RES, -1, HD),
                pool_keys.reshape(-1, PAGE, HD),
                pool_values.reshape(-1, PAGE, HD),
                out_weight,
            )
        )
    )


def solution(mesh):
    heads = P("inst", "tp", None, None)
    in_specs = (heads,) * 7 + (P(),) * 6 + (P("tp", None),)
    return jax.shard_map(
        per_device, mesh=mesh, in_specs=in_specs, out_specs=P("inst", "tp"), check_vma=False
    )
```

```python
import math

import jax
import jax.numpy as jnp
from jax import lax
from jax.experimental import pallas as pl
from jax.experimental.pallas import tpu as pltpu
from jax.sharding import PartitionSpec as P

MESH = pl.DeviceIdType.MESH
NX, NZ, NY = 2, 8, 4
PEERS = NX * NY
TP = 4
RES, NEW, MIG = 6, 4, 2
STEPS = 4
ROWS = 32
HD = 128
PAGE = 128
NPAGES = 16
LOW = -1e30
NT = (((1,), (1,)), ((), ()))
NN = (((1,), (0,)), ((), ()))


def mirror(r):
    dx, dy = divmod(r, NY)
    return dx * NY + (NY - dy) % NY


def iota(shape, axis):
    return lax.broadcasted_iota(jnp.int32, shape, axis)


def dot(a, b, dims=NN):
    return lax.dot_general(a, b, dims, preferred_element_type=jnp.float32)


def kernel(
    res_len_in,
    new_len_in,
    partner_bit_in,
    migrate_out_in,
    page_source_in,
    page_index_in,
    queries_in,
    new_keys_in,
    new_values_in,
    res_keys,
    res_values,
    pool_keys,
    pool_values,
    weight,
    out,
    res_len,
    new_len,
    partner_bit,
    migrate_out,
    page_source,
    page_index,
    queries,
    new_keys,
    new_values,
    rk,
    rv,
    pk,
    pv,
    wv,
    tab_v,
    tab,
    q1,
    fw,
    q2,
    r1s,
    r1,
    sts,
    st,
    r2s,
    ls,
    fin,
    lf,
    att,
    guest,
    attm,
    xres,
    xnew,
    own1,
    own2,
    rs1s,
    rs1,
    rs2s,
    rs2,
    load_sem,
    q1_send,
    q1_recv,
    q2_send,
    q2_recv,
    r1_send,
    r1_recv,
    st_send,
    st_recv,
    r2_send,
    r2_recv,
    lf_send,
    lf_recv,
    mig_send,
    mig_recv,
    rs1_send,
    rs1_recv,
    rs2_send,
    rs2_recv,
):
    me = lax.axis_index("inst")
    tp = lax.axis_index("tp")
    y = lax.rem(me, NY)
    z = lax.rem(lax.div(me, NY), NZ)
    x = lax.div(me, NY * NZ)
    hi = lax.div(tp, 2)
    core = lax.rem(tp, 2)
    scale = 1.0 / math.sqrt(HD)

    def inst_at(xx, zz, yy):
        return (xx * NZ + zz) * NY + yy

    def plane(r, zz):
        dx, dy = divmod(r, NY)
        return inst_at(lax.rem(x + dx, NX), zz, lax.rem(y + dy, NY))

    def line(zi):
        return inst_at(x, lax.rem(z + zi, NZ), y)

    bases = [plane(r, 0) for r in range(PEERS)]
    peers = [base + z * NY for base in bases]

    def tp_peer(o):
        return lax.rem(hi + o // 2, 2) * 2 + lax.rem(core + o % 2, 2)

    def order(i):
        odd = lax.rem(i, 2)
        return lax.rem(odd * lax.div(i + 1, 2) + (1 - odd) * (NZ - lax.div(i, 2)), NZ)

    def remote(src, dst, send, recv, inst, t=tp):
        return pltpu.make_async_remote_copy(
            src_ref=src,
            dst_ref=dst,
            send_sem=send,
            recv_sem=recv,
            device_id=(inst, t),
            device_id_type=MESH,
        )

    def drain(ref, sem):
        pltpu.make_async_copy(ref, ref, sem).wait()

    loads = [
        pltpu.make_async_copy(src, dst, load_sem.at[k])
        for k, (src, dst) in enumerate(
            [
                (res_keys, rk),
                (res_values, rv),
                (pool_keys, pk),
                (pool_values, pv),
                (weight, wv),
                (page_source_in, page_source),
                (page_index_in, page_index),
                (queries_in, queries),
                (new_keys_in, new_keys),
                (new_values_in, new_values),
                (res_len_in, res_len),
                (new_len_in, new_len),
                (partner_bit_in, partner_bit),
                (migrate_out_in, migrate_out),
            ]
        )
    ]
    for k in (5, 6, 7, 11, 10, 8, 9, 12, 13, 0, 1, 2, 3, 4):
        loads[k].start()

    barrier = pltpu.get_barrier_semaphore()
    for zi in range(1, NZ):
        pl.semaphore_signal(barrier, inc=1, device_id=(line(zi), tp), device_id_type=MESH)
    for r in range(1, PEERS):
        pl.semaphore_signal(barrier, inc=1, device_id=(peers[r], tp), device_id_type=MESH)
    for o in range(1, TP):
        pl.semaphore_signal(barrier, inc=1, device_id=(me, tp_peer(o)), device_id_type=MESH)
    pl.semaphore_wait(barrier, NZ - 1 + PEERS - 1 + TP - 1)

    seq = [0, 1, 7, 2, 6, 3, 5, 4]
    q1_copies = []
    for i in range(1, NZ):
        zi = seq[i]
        back = seq.index(NZ - zi)
        copy = remote(
            queries_in.at[pl.ds(RES * ROWS, NEW * ROWS)],
            q1.at[back],
            q1_send.at[i],
            q1_recv.at[back],
            line(zi),
        )
        copy.start()
        q1_copies.append(copy)
    loads[5].wait()
    loads[6].wait()
    places = page_source.shape[1]
    count = page_source.shape[0]
    source = page_source[...]
    slot = page_index[...]
    place = iota((count, places), 1)
    lane = iota((count, HD), 1)
    table = jnp.zeros((count, HD), jnp.int32)
    for r in range(PEERS):
        hit = source == peers[r]
        first = jnp.min(jnp.where(hit, place, places), axis=1, keepdims=True)
        last = jnp.max(jnp.where(hit, place, -1), axis=1, keepdims=True)
        last = jnp.where(last > first, last, places)
        for c, p in ((0, first), (1, last)):
            table = jnp.where(lane == 2 * r + c, lax.shift_right_logical(p, NPAGES.bit_length() - 1), table)
            if r == 0:
                page = jnp.max(jnp.where(place == p, slot, 0), axis=1, keepdims=True)
                table = jnp.where(lane == 2 * PEERS + c, page, table)
                skip = (p & (NPAGES - 1)) * PAGE
                table = jnp.where(lane == 2 * PEERS + 2 + c, skip, table)
    tab_v[...] = table
    tab_copy = pltpu.make_async_copy(tab_v, tab, load_sem.at[14])
    tab_copy.start()

    loads[7].wait()
    q1[0] = queries[RES * ROWS :, :]

    def forward(i):
        dest = line(order(i))
        block = [q1[i, pl.ds(n * ROWS, ROWS), :] for n in range(NEW)]
        for r in range(PEERS):
            for c in range(2):
                n = tab[dest, 2 * r + c]
                q = lax.select(
                    n == 0,
                    block[0],
                    lax.select(n == 1, block[1], lax.select(n == 2, block[2], block[3])),
                )
                if r == 0:
                    q2[i, 0, pl.ds(c * ROWS, ROWS), :] = q
                else:
                    fw[i, r, pl.ds(c * ROWS, ROWS), :] = q
            if r > 0:
                remote(
                    fw.at[i, r], q2.at[i, mirror(r)], q2_send.at[i], q2_recv.at[i], peers[r]
                ).start()

    tab_copy.wait()
    forward(jnp.int32(0))

    def forward_step(i, carry):
        drain(q1.at[i], q1_recv.at[i])
        forward(i)
        return carry

    lax.fori_loop(1, NZ, forward_step, 0)

    for k in range(8, 14):
        loads[k].wait()
    fresh_count = new_keys.shape[0]
    fresh_k = new_keys[...]
    fresh_v = new_values[...]
    diag = iota((ROWS, HD), 0) == lax.rem(iota((ROWS, HD), 1), ROWS)

    def fresh_scores(request, q):
        s = dot(q, fresh_k, NT) * scale
        row = iota((ROWS, fresh_count), 0)
        col = iota((ROWS, fresh_count), 1)
        live = (lax.div(col, STEPS) == request) & (lax.rem(col, STEPS) <= lax.rem(row, STEPS))
        return jnp.where(live, s, LOW)

    def as_row(column):
        return jnp.sum(jnp.where(diag, column, 0.0), axis=0, keepdims=True)

    quarter = lax.div(iota((1, HD), 1), ROWS)
    for n in range(NEW):
        s = fresh_scores(RES + n, queries[pl.ds((RES + n) * ROWS, ROWS), :])
        m = jnp.max(s, axis=1, keepdims=True)
        p = jnp.exp(s - m)
        l = jnp.sum(p, axis=1, keepdims=True)
        fin[n, 0] = (dot(p.astype(jnp.bfloat16), fresh_v) / l).astype(jnp.bfloat16)
        lf[0, pl.ds(n, 1), :] = as_row(m + jnp.log(l))

    loads[0].wait()
    loads[1].wait()
    context = rk.shape[1]

    def resident_step(i, carry):
        for half in range(2):
            request = 2 * i + half
            q = queries[pl.ds(pl.multiple_of(request * ROWS, ROWS), ROWS), :]
            s = dot(q, rk[request], NT) * scale
            s = jnp.where(iota((ROWS, context), 1) < res_len[me * RES + request], s, LOW)
            f = fresh_scores(request, q)
            m = jnp.maximum(
                jnp.max(s, axis=1, keepdims=True), jnp.max(f, axis=1, keepdims=True)
            )
            p = jnp.exp(s - m)
            g = jnp.exp(f - m)
            l = jnp.sum(p, axis=1, keepdims=True) + jnp.sum(g, axis=1, keepdims=True)
            o = dot(p.astype(jnp.bfloat16), rv[request]) + dot(g.astype(jnp.bfloat16), fresh_v)
            att[pl.ds(pl.multiple_of(request * ROWS, ROWS), ROWS), :] = (o / l).astype(
                jnp.bfloat16
            )
        return carry

    lax.fori_loop(0, RES // 2, resident_step, 0)
    partners = [
        inst_at(x, z, y + 1 - 2 * lax.rem(y, 2)),
        inst_at(x, z, lax.rem(y + 2, NY)),
    ]
    mig_copies = []
    for bit in range(2):
        copy = remote(
            att.at[pl.ds((RES - MIG) * ROWS, MIG * ROWS)],
            guest.at[bit],
            mig_send.at[bit],
            mig_recv.at[bit],
            partners[bit],
        )
        copy.start()
        mig_copies.append(copy)

    loads[2].wait()
    loads[3].wait()
    low_half = lax.rem(lax.div(iota((1, HD), 1), ROWS), 2) == 0
    tile_row = iota((2 * NEW, HD), 0)
    key_lane = iota((ROWS, PAGE), 1)

    def send_part(i, r):
        remote(
            r1s.at[i, r], r1.at[i, mirror(r)], r1_send.at[i], r1_recv.at[i], peers[r]
        ).start()

    def send_level(ip, r):
        remote(
            sts.at[ip, r], st.at[ip, mirror(r)], st_send.at[ip], st_recv.at[ip], peers[r]
        ).start()

    def partial_pair(ip, send, halves=(0, 1)):
        tiles = [jnp.full((2 * NEW, HD), LOW, jnp.float32) for _ in range(PEERS)]
        for half in halves:
            i = 2 * ip + half
            drain(q2.at[i, pl.ds(1, PEERS - 1)], q2_recv.at[i])
            dest_z = lax.rem(z + order(i), NZ)
            for base in range(0, PEERS, 8):
                scores, values, request = [], [], []
                for r in range(base, base + 8):
                    dest = bases[r] + dest_z * NY
                    for c in range(2):
                        n = tab[dest, c]
                        page = tab[dest, 2 * PEERS + c]
                        length = new_len[dest * NEW + jnp.minimum(n, NEW - 1)]
                        live = length - tab[dest, 2 * PEERS + 2 + c]
                        s = dot(q2[i, r, pl.ds(c * ROWS, ROWS), :], pk[page], NT) * scale
                        scores.append(jnp.where(key_lane < live, s, LOW))
                        values.append(pv[page])
                        request.append(n)
                tops = [jnp.max(s, axis=1, keepdims=True) for s in scores]
                exps = [jnp.exp(s - m) for s, m in zip(scores, tops)]
                sums = [jnp.sum(p, axis=1, keepdims=True) for p in exps]
                outs = [
                    (dot(p.astype(jnp.bfloat16), v) / l).astype(jnp.bfloat16)
                    for p, v, l in zip(exps, values, sums)
                ]
                rows = [as_row(m + jnp.log(l)) for m, l in zip(tops, sums)]
                for k, r in enumerate(range(base, base + 8)):
                    for c in range(2):
                        if r == 0:
                            r1[i, 0, pl.ds(c * ROWS, ROWS), :] = outs[2 * k + c]
                        else:
                            r1s[i, r, pl.ds(c * ROWS, ROWS), :] = outs[2 * k + c]
                    level = jnp.where(low_half, rows[2 * k], rows[2 * k + 1])
                    wanted = jnp.where(low_half, request[2 * k], request[2 * k + 1]) + half * NEW
                    filled = jnp.where(low_half, request[2 * k], request[2 * k + 1]) < NEW
                    tiles[r] = jnp.where((tile_row == wanted) & filled, level, tiles[r])
                    if r > 0 and send:
                        send_part(i, r)
        for r in range(PEERS):
            if r == 0:
                st[ip, 0] = tiles[0]
            else:
                sts[ip, r] = tiles[r]
                if send:
                    send_level(ip, r)

    def partial_step(ip, carry):
        partial_pair(ip, True)
        return carry

    lax.fori_loop(1, NZ // 2, partial_step, 0)
    partial_pair(jnp.int32(0), True, (1, 0))

    for copy in mig_copies:
        copy.wait()
    bit = partner_bit[me]
    hand_here = migrate_out[me]
    hand_there = lax.select(bit == 0, migrate_out[partners[0]], migrate_out[partners[1]])
    nothing = jnp.zeros((ROWS, HD), jnp.bfloat16)
    for r in range(RES):
        attm[pl.ds(r * ROWS, ROWS), :] = lax.select(
            r < RES - hand_here, att[pl.ds(r * ROWS, ROWS), :], nothing
        )
    for m in range(MIG):
        came = lax.select(
            bit == 0, guest[0, pl.ds(m * ROWS, ROWS), :], guest[1, pl.ds(m * ROWS, ROWS), :]
        )
        attm[pl.ds((RES + m) * ROWS, ROWS), :] = lax.select(
            m >= MIG - hand_there, came, nothing
        )

    def by_head(values, slots):
        size = slots * ROWS
        row = iota((size, size), 0)
        col = iota((size, size), 1)
        goal = (
            lax.rem(lax.div(row, STEPS), slots) * ROWS
            + lax.div(row, STEPS * slots) * STEPS
            + lax.rem(row, STEPS)
        )
        moved = dot(jnp.where(col == goal, 1.0, 0.0).astype(jnp.bfloat16), values)
        return moved.astype(jnp.bfloat16)

    moved = by_head(attm[...], RES + MIG)
    lead = (RES + MIG) * STEPS
    for h in range(ROWS // STEPS):
        xres[:, pl.ds(h * HD, HD)] = moved[h * lead : (h + 1) * lead]
    loads[4].wait()
    width = out.shape[1]

    def project(rows_ref, sends, send_sem, recv, recv_sem, own):
        copies = []
        for o in (3, 2, 1, 0):
            peer = tp_peer(o)
            part = dot(rows_ref[...], wv[:, pl.ds(pl.multiple_of(peer * width, width), width)])
            if o == 0:
                own[...] = part
            else:
                sends[o] = part.astype(jnp.bfloat16)
                copy = remote(sends.at[o], recv.at[o], send_sem.at[o], recv_sem.at[o], me, peer)
                copy.start()
                copies.append(copy)
        return copies

    rs1_copies = project(xres, rs1s, rs1_send, rs1, rs1_recv, own1)

    low = iota((2 * NEW, HD), 1) < 2 * ROWS

    def pair_levels(ip):
        drain(st.at[ip, pl.ds(1, PEERS - 1)], st_recv.at[ip])
        return [
            jnp.where(low, st[ip, 2 * q], st[ip, 2 * q + 1]) for q in range(PEERS // 2)
        ]

    def softmax_over(levels):
        m = levels[0]
        for level in levels[1:]:
            m = jnp.maximum(m, level)
        m = jnp.maximum(m, pltpu.roll(m, 2 * ROWS, 1))
        m = jnp.maximum(m, pltpu.roll(m, ROWS, 1))
        shares = [jnp.exp(level - m) for level in levels]
        total = shares[0]
        for share in shares[1:]:
            total = total + share
        total = total + pltpu.roll(total, 2 * ROWS, 1)
        total = total + pltpu.roll(total, ROWS, 1)
        return [share / total for share in shares], m + jnp.log(total)

    def merge(ip, levels, halves):
        shares, together = softmax_over(levels)
        ls[ip] = together
        for half in halves:
            i = 2 * ip + half
            drain(r1.at[i, pl.ds(1, PEERS - 1)], r1_recv.at[i])
            blocks = []
            for n in range(NEW):
                k = half * NEW + n
                blocks.append(
                    jnp.concatenate(
                        [jnp.where(diag, share[k : k + 1], 0.0) for share in shares], axis=1
                    )
                )
            mix = jnp.concatenate(blocks, axis=0).astype(jnp.bfloat16)
            merged = dot(mix, r1[i].reshape(PEERS * 2 * ROWS, HD)).astype(jnp.bfloat16)
            for n in range(NEW):
                r2s[i, n] = merged[n * ROWS : (n + 1) * ROWS]
            zi = order(i)
            turned = i + 1 - 2 * lax.rem(i + 1, 2)
            back = turned - lax.div(turned, NZ)
            remote(
                r2s.at[i], fin.at[:, back], r2_send.at[i], r2_recv.at[back], line(zi)
            ).start()
            remote(ls.at[ip], lf.at[back], lf_send.at[i], lf_recv.at[back], line(zi)).start()

    def merge_step(ip, carry):
        merge(ip, pair_levels(ip), (0, 1))
        return carry

    lax.fori_loop(1, NZ // 2, merge_step, 0)
    near = pair_levels(0)
    merge(jnp.int32(0), near, (1,))

    drain(r1.at[0, pl.ds(1, PEERS - 1)], r1_recv.at[0])
    for i in range(1, NZ):
        drain(lf.at[i], lf_recv.at[i])
        drain(fin.at[:, i], r2_recv.at[i])
    from_odd = [False, False, True, False, True, False, True, True]
    levels = [level[:NEW] for level in near]
    for base in range(0, NZ, 4):
        level = jnp.full((NEW, HD), LOW, jnp.float32)
        for g in range(4):
            i = base + g
            rows = lf[i, pl.ds(NEW if from_odd[i] else 0, NEW), :]
            level = jnp.where(quarter == g, rows, level)
        levels.append(level)
    shares, _ = softmax_over(levels)
    tail = NEW * STEPS
    row = iota((tail, HD), 0)
    spread = []
    for share in shares:
        wide = jnp.zeros((tail, HD), jnp.float32)
        for n in range(NEW):
            wide = jnp.where(lax.div(row, STEPS) == n, share[n : n + 1], wide)
        spread.append(wide)
    column = lax.rem(iota((tail, HD), 1), ROWS) - lax.rem(row, STEPS)
    owner = lax.div(row, STEPS)

    def mixing(parts, n):
        rows = []
        for h in range(ROWS // STEPS):
            keep = column == h * STEPS
            if n is not None:
                keep = keep & (owner == n)
            rows.append(
                jnp.concatenate([jnp.where(keep, part, 0.0) for part in parts], axis=1)
            )
        return jnp.concatenate(rows, axis=0).astype(jnp.bfloat16)

    attended = dot(mixing(spread[: PEERS // 2], None), r1[0].reshape(PEERS * 2 * ROWS, HD))
    for n in range(NEW):
        attended = attended + dot(
            mixing(spread[PEERS // 2 :], n), fin[n].reshape(NZ * ROWS, HD)
        )
    attended = attended.astype(jnp.bfloat16)
    for h in range(ROWS // STEPS):
        xnew[:, pl.ds(h * HD, HD)] = attended[h * tail : (h + 1) * tail]
    rs2_copies = project(xnew, rs2s, rs2_send, rs2, rs2_recv, own2)

    for copy in rs1_copies:
        copy.wait()
    total = own1[...]
    for o in range(1, TP):
        total = total + rs1[o].astype(jnp.float32)
    out[pl.ds(0, lead), :] = total.astype(jnp.bfloat16)
    for copy in q1_copies:
        copy.wait_send()
    for i in range(NZ):
        drain(fw.at[i, pl.ds(1, PEERS - 1)], q2_send.at[i])
        drain(r1s.at[i, pl.ds(1, PEERS - 1)], r1_send.at[i])
        if i > 0:
            drain(r2s.at[i], r2_send.at[i])
            drain(ls.at[i // 2], lf_send.at[i])
    for ip in range(NZ // 2):
        drain(sts.at[ip, pl.ds(1, PEERS - 1)], st_send.at[ip])
    for copy in rs2_copies:
        copy.wait()
    total = own2[...]
    for o in range(1, TP):
        total = total + rs2[o].astype(jnp.float32)
    out[pl.ds(lead, tail), :] = total.astype(jnp.bfloat16)


def per_device(
    res_keys,
    res_values,
    pool_keys,
    pool_values,
    queries,
    new_keys,
    new_values,
    res_len,
    new_len,
    page_source,
    page_index,
    partner_bit,
    migrate_out,
    out_weight,
):
    bf, f32 = jnp.bfloat16, jnp.float32
    rows = (RES + MIG + NEW) * STEPS
    lead, tail = (RES + MIG) * STEPS, NEW * STEPS
    width = out_weight.shape[1] // TP
    vmem = pl.BlockSpec(memory_space=pltpu.VMEM)
    hbm = pl.BlockSpec(memory_space=pltpu.HBM)
    dma = pltpu.SemaphoreType.DMA
    depth = out_weight.shape[0]
    whole = [
        pltpu.SMEM(res_len.shape, jnp.int32),
        pltpu.SMEM(new_len.shape, jnp.int32),
        pltpu.SMEM(partner_bit.shape, jnp.int32),
        pltpu.SMEM(migrate_out.shape, jnp.int32),
        pltpu.VMEM(page_source.shape, jnp.int32),
        pltpu.VMEM(page_index.shape, jnp.int32),
        pltpu.VMEM((queries.shape[0] * ROWS, HD), bf),
        pltpu.VMEM((queries.shape[0] * STEPS, HD), bf),
        pltpu.VMEM((queries.shape[0] * STEPS, HD), bf),
    ]
    scratch = whole + [
        pltpu.VMEM((RES, res_keys.shape[2], HD), bf),
        pltpu.VMEM((RES, res_keys.shape[2], HD), bf),
        pltpu.VMEM((pool_keys.shape[0], PAGE, HD), bf),
        pltpu.VMEM((pool_keys.shape[0], PAGE, HD), bf),
        pltpu.VMEM(out_weight.shape, bf),
        pltpu.VMEM((page_source.shape[0], HD), jnp.int32),
        pltpu.SMEM((page_source.shape[0], HD), jnp.int32),
        pltpu.VMEM((NZ, NEW * ROWS, HD), bf),
        pltpu.VMEM((NZ, PEERS, 2 * ROWS, HD), bf),
        pltpu.VMEM((NZ, PEERS, 2 * ROWS, HD), bf),
        pltpu.VMEM((NZ, PEERS, 2 * ROWS, HD), bf),
        pltpu.VMEM((NZ, PEERS, 2 * ROWS, HD), bf),
        pltpu.VMEM((NZ // 2, PEERS, 2 * NEW, HD), f32),
        pltpu.VMEM((NZ // 2, PEERS, 2 * NEW, HD), f32),
        pltpu.VMEM((NZ, NEW, ROWS, HD), bf),
        pltpu.VMEM((NZ // 2, 2 * NEW, HD), f32),
        pltpu.VMEM((NEW, NZ, ROWS, HD), bf),
        pltpu.VMEM((NZ, 2 * NEW, HD), f32),
        pltpu.VMEM((RES * ROWS, HD), bf),
        pltpu.VMEM((2, MIG * ROWS, HD), bf),
        pltpu.VMEM(((RES + MIG) * ROWS, HD), bf),
        pltpu.VMEM((lead, depth), bf),
        pltpu.VMEM((tail, depth), bf),
        pltpu.VMEM((lead, width), f32),
        pltpu.VMEM((tail, width), f32),
        pltpu.VMEM((TP, lead, width), bf),
        pltpu.VMEM((TP, lead, width), bf),
        pltpu.VMEM((TP, tail, width), bf),
        pltpu.VMEM((TP, tail, width), bf),
        dma((15,)),
        dma((NZ,)),
        dma((NZ,)),
        dma((NZ,)),
        dma((NZ,)),
        dma((NZ,)),
        dma((NZ,)),
        dma((NZ // 2,)),
        dma((NZ // 2,)),
        dma((NZ,)),
        dma((NZ,)),
        dma((NZ,)),
        dma((NZ,)),
        dma((2,)),
        dma((2,)),
        dma((TP,)),
        dma((TP,)),
        dma((TP,)),
        dma((TP,)),
    ]
    return pl.pallas_call(
        kernel,
        out_shape=jax.ShapeDtypeStruct((rows, width), bf),
        in_specs=[hbm] * 14,
        out_specs=vmem,
        scratch_shapes=scratch,
        compiler_params=pltpu.CompilerParams(
            collective_id=0, has_side_effects=True, vmem_limit_bytes=48 * 2**20
        ),
        cost_estimate=pl.CostEstimate(
            flops=10**9, bytes_accessed=16 * 2**20, transcendentals=10**6
        ),
    )(
        *(
            pltpu.with_memory_space_constraint(operand, pltpu.HBM)
            for operand in (
                res_len,
                new_len,
                partner_bit,
                migrate_out,
                page_source,
                page_index,
                queries.reshape(-1, HD),
                new_keys.reshape(-1, HD),
                new_values.reshape(-1, HD),
                res_keys.reshape(RES, -1, HD),
                res_values.reshape(RES, -1, HD),
                pool_keys.reshape(-1, PAGE, HD),
                pool_values.reshape(-1, PAGE, HD),
                out_weight,
            )
        )
    )


def solution(mesh):
    heads = P("inst", "tp", None, None)
    in_specs = (heads,) * 7 + (P(),) * 6 + (P("tp", None),)
    return jax.shard_map(
        per_device, mesh=mesh, in_specs=in_specs, out_specs=P("inst", "tp"), check_vma=False
    )
```

```python
import math

import jax
import jax.numpy as jnp
from jax import lax
from jax.experimental import pallas as pl
from jax.experimental.pallas import tpu as pltpu
from jax.sharding import PartitionSpec as P

MESH = pl.DeviceIdType.MESH
NX, NZ, NY = 2, 8, 4
PEERS = NX * NY
TP = 4
RES, NEW, MIG = 6, 4, 2
STEPS = 4
ROWS = 32
HD = 128
PAGE = 128
NPAGES = 16
LOW = -1e30
NT = (((1,), (1,)), ((), ()))
NN = (((1,), (0,)), ((), ()))


def mirror(r):
    dx, dy = divmod(r, NY)
    return dx * NY + (NY - dy) % NY


def iota(shape, axis):
    return lax.broadcasted_iota(jnp.int32, shape, axis)


def dot(a, b, dims=NN):
    return lax.dot_general(a, b, dims, preferred_element_type=jnp.float32)


def kernel(
    res_len_in,
    new_len_in,
    partner_bit_in,
    migrate_out_in,
    page_source_in,
    page_index_in,
    queries_in,
    new_keys_in,
    new_values_in,
    res_keys,
    res_values,
    pool_keys,
    pool_values,
    weight,
    out,
    res_len,
    new_len,
    partner_bit,
    migrate_out,
    page_source,
    page_index,
    queries,
    new_keys,
    new_values,
    rk,
    rv,
    pk,
    pv,
    wv,
    tab_v,
    tab,
    q1,
    fw,
    q2,
    r1s,
    r1,
    sts,
    st,
    r2s,
    ls,
    fin,
    lf,
    att,
    guest,
    attm,
    xres,
    xnew,
    own1,
    own2,
    rs1s,
    rs1,
    rs2s,
    rs2,
    load_sem,
    q1_send,
    q1_recv,
    q2_send,
    q2_recv,
    r1_send,
    r1_recv,
    st_send,
    st_recv,
    r2_send,
    r2_recv,
    lf_send,
    lf_recv,
    mig_send,
    mig_recv,
    rs1_send,
    rs1_recv,
    rs2_send,
    rs2_recv,
):
    me = lax.axis_index("inst")
    tp = lax.axis_index("tp")
    y = lax.rem(me, NY)
    z = lax.rem(lax.div(me, NY), NZ)
    x = lax.div(me, NY * NZ)
    hi = lax.div(tp, 2)
    core = lax.rem(tp, 2)
    scale = 1.0 / math.sqrt(HD)

    def inst_at(xx, zz, yy):
        return (xx * NZ + zz) * NY + yy

    def plane(r, zz):
        dx, dy = divmod(r, NY)
        return inst_at(lax.rem(x + dx, NX), zz, lax.rem(y + dy, NY))

    def line(zi):
        return inst_at(x, lax.rem(z + zi, NZ), y)

    bases = [plane(r, 0) for r in range(PEERS)]
    peers = [base + z * NY for base in bases]

    def tp_peer(o):
        return lax.rem(hi + o // 2, 2) * 2 + lax.rem(core + o % 2, 2)

    def order(i):
        odd = lax.rem(i, 2)
        return lax.rem(odd * lax.div(i + 1, 2) + (1 - odd) * (NZ - lax.div(i, 2)), NZ)

    def remote(src, dst, send, recv, inst, t=tp):
        return pltpu.make_async_remote_copy(
            src_ref=src,
            dst_ref=dst,
            send_sem=send,
            recv_sem=recv,
            device_id=(inst, t),
            device_id_type=MESH,
        )

    def drain(ref, sem):
        pltpu.make_async_copy(ref, ref, sem).wait()

    loads = [
        pltpu.make_async_copy(src, dst, load_sem.at[k])
        for k, (src, dst) in enumerate(
            [
                (res_keys, rk),
                (res_values, rv),
                (pool_keys, pk),
                (pool_values, pv),
                (weight, wv),
                (page_source_in, page_source),
                (page_index_in, page_index),
                (queries_in, queries),
                (new_keys_in, new_keys),
                (new_values_in, new_values),
                (res_len_in, res_len),
                (new_len_in, new_len),
                (partner_bit_in, partner_bit),
                (migrate_out_in, migrate_out),
            ]
        )
    ]
    for k in (5, 6, 7, 11, 10, 8, 9, 12, 13, 0, 1, 2, 3, 4):
        loads[k].start()

    barrier = pltpu.get_barrier_semaphore()
    for zi in range(1, NZ):
        pl.semaphore_signal(barrier, inc=1, device_id=(line(zi), tp), device_id_type=MESH)
    for r in range(1, PEERS):
        pl.semaphore_signal(barrier, inc=1, device_id=(peers[r], tp), device_id_type=MESH)
    for o in range(1, TP):
        pl.semaphore_signal(barrier, inc=1, device_id=(me, tp_peer(o)), device_id_type=MESH)
    loads[5].wait()
    loads[6].wait()
    places = page_source.shape[1]
    count = page_source.shape[0]
    source = page_source[...]
    slot = page_index[...]
    place = iota((count, places), 1)
    lane = iota((count, HD), 1)
    table = jnp.zeros((count, HD), jnp.int32)
    for r in range(PEERS):
        hit = source == peers[r]
        first = jnp.min(jnp.where(hit, place, places), axis=1, keepdims=True)
        last = jnp.max(jnp.where(hit, place, -1), axis=1, keepdims=True)
        last = jnp.where(last > first, last, places)
        for c, p in ((0, first), (1, last)):
            table = jnp.where(lane == 2 * r + c, lax.shift_right_logical(p, NPAGES.bit_length() - 1), table)
            if r == 0:
                page = jnp.max(jnp.where(place == p, slot, 0), axis=1, keepdims=True)
                table = jnp.where(lane == 2 * PEERS + c, page, table)
                skip = (p & (NPAGES - 1)) * PAGE
                table = jnp.where(lane == 2 * PEERS + 2 + c, skip, table)
    tab_v[...] = table
    tab_copy = pltpu.make_async_copy(tab_v, tab, load_sem.at[14])
    tab_copy.start()

    pl.semaphore_wait(barrier, NZ - 1 + PEERS - 1 + TP - 1)

    seq = [0, 1, 7, 2, 6, 3, 5, 4]
    q1_copies = []
    loads[7].wait()
    for i in range(1, NZ):
        zi = seq[i]
        back = seq.index(NZ - zi)
        copy = remote(
            queries.at[pl.ds(RES * ROWS, NEW * ROWS)],
            q1.at[back],
            q1_send.at[i],
            q1_recv.at[back],
            line(zi),
        )
        copy.start()
        q1_copies.append(copy)
    q1[0] = queries[RES * ROWS :, :]

    def forward(i):
        dest = line(order(i))
        block = [q1[i, pl.ds(n * ROWS, ROWS), :] for n in range(NEW)]
        for r in range(PEERS):
            for c in range(2):
                n = tab[dest, 2 * r + c]
                q = lax.select(
                    n == 0,
                    block[0],
                    lax.select(n == 1, block[1], lax.select(n == 2, block[2], block[3])),
                )
                if r == 0:
                    q2[i, 0, pl.ds(c * ROWS, ROWS), :] = q
                else:
                    fw[i, r, pl.ds(c * ROWS, ROWS), :] = q
            if r > 0:
                remote(
                    fw.at[i, r], q2.at[i, mirror(r)], q2_send.at[i], q2_recv.at[i], peers[r]
                ).start()

    tab_copy.wait()
    forward(jnp.int32(0))

    def forward_step(i, carry):
        drain(q1.at[i], q1_recv.at[i])
        forward(i)
        return carry

    lax.fori_loop(1, NZ, forward_step, 0)

    for k in range(8, 14):
        loads[k].wait()
    fresh_count = new_keys.shape[0]
    fresh_k = new_keys[...]
    fresh_v = new_values[...]
    diag = iota((ROWS, HD), 0) == lax.rem(iota((ROWS, HD), 1), ROWS)

    def fresh_scores(request, q):
        s = dot(q, fresh_k, NT) * scale
        row = iota((ROWS, fresh_count), 0)
        col = iota((ROWS, fresh_count), 1)
        live = (lax.div(col, STEPS) == request) & (lax.rem(col, STEPS) <= lax.rem(row, STEPS))
        return jnp.where(live, s, LOW)

    def as_row(column):
        return jnp.sum(jnp.where(diag, column, 0.0), axis=0, keepdims=True)

    quarter = lax.div(iota((1, HD), 1), ROWS)
    for n in range(NEW):
        s = fresh_scores(RES + n, queries[pl.ds((RES + n) * ROWS, ROWS), :])
        m = jnp.max(s, axis=1, keepdims=True)
        p = jnp.exp(s - m)
        l = jnp.sum(p, axis=1, keepdims=True)
        fin[n, 0] = (dot(p.astype(jnp.bfloat16), fresh_v) / l).astype(jnp.bfloat16)
        lf[0, pl.ds(n, 1), :] = as_row(m + jnp.log(l))

    loads[0].wait()
    loads[1].wait()
    context = rk.shape[1]

    def resident_step(i, carry):
        for half in range(2):
            request = 2 * i + half
            q = queries[pl.ds(pl.multiple_of(request * ROWS, ROWS), ROWS), :]
            s = dot(q, rk[request], NT) * scale
            s = jnp.where(iota((ROWS, context), 1) < res_len[me * RES + request], s, LOW)
            f = fresh_scores(request, q)
            m = jnp.maximum(
                jnp.max(s, axis=1, keepdims=True), jnp.max(f, axis=1, keepdims=True)
            )
            p = jnp.exp(s - m)
            g = jnp.exp(f - m)
            l = jnp.sum(p, axis=1, keepdims=True) + jnp.sum(g, axis=1, keepdims=True)
            o = dot(p.astype(jnp.bfloat16), rv[request]) + dot(g.astype(jnp.bfloat16), fresh_v)
            att[pl.ds(pl.multiple_of(request * ROWS, ROWS), ROWS), :] = (o / l).astype(
                jnp.bfloat16
            )
        return carry

    lax.fori_loop(0, RES // 2, resident_step, 0)
    partners = [
        inst_at(x, z, y + 1 - 2 * lax.rem(y, 2)),
        inst_at(x, z, lax.rem(y + 2, NY)),
    ]
    mig_copies = []
    for bit in range(2):
        copy = remote(
            att.at[pl.ds((RES - MIG) * ROWS, MIG * ROWS)],
            guest.at[bit],
            mig_send.at[bit],
            mig_recv.at[bit],
            partners[bit],
        )
        copy.start()
        mig_copies.append(copy)

    loads[2].wait()
    loads[3].wait()
    low_half = lax.rem(lax.div(iota((1, HD), 1), ROWS), 2) == 0
    tile_row = iota((2 * NEW, HD), 0)
    key_lane = iota((ROWS, PAGE), 1)

    def send_part(i, r):
        remote(
            r1s.at[i, r], r1.at[i, mirror(r)], r1_send.at[i], r1_recv.at[i], peers[r]
        ).start()

    def send_level(ip, r):
        remote(
            sts.at[ip, r], st.at[ip, mirror(r)], st_send.at[ip], st_recv.at[ip], peers[r]
        ).start()

    def partial_pair(ip, send, halves=(0, 1)):
        tiles = [jnp.full((2 * NEW, HD), LOW, jnp.float32) for _ in range(PEERS)]
        for half in halves:
            i = 2 * ip + half
            drain(q2.at[i, pl.ds(1, PEERS - 1)], q2_recv.at[i])
            dest_z = lax.rem(z + order(i), NZ)
            for base in range(0, PEERS, 8):
                scores, values, request = [], [], []
                for r in range(base, base + 8):
                    dest = bases[r] + dest_z * NY
                    for c in range(2):
                        n = tab[dest, c]
                        page = tab[dest, 2 * PEERS + c]
                        length = new_len[dest * NEW + jnp.minimum(n, NEW - 1)]
                        live = length - tab[dest, 2 * PEERS + 2 + c]
                        s = dot(q2[i, r, pl.ds(c * ROWS, ROWS), :], pk[page], NT) * scale
                        scores.append(jnp.where(key_lane < live, s, LOW))
                        values.append(pv[page])
                        request.append(n)
                tops = [jnp.max(s, axis=1, keepdims=True) for s in scores]
                exps = [jnp.exp(s - m) for s, m in zip(scores, tops)]
                sums = [jnp.sum(p, axis=1, keepdims=True) for p in exps]
                outs = [
                    (dot(p.astype(jnp.bfloat16), v) / l).astype(jnp.bfloat16)
                    for p, v, l in zip(exps, values, sums)
                ]
                rows = [as_row(m + jnp.log(l)) for m, l in zip(tops, sums)]
                for k, r in enumerate(range(base, base + 8)):
                    for c in range(2):
                        if r == 0:
                            r1[i, 0, pl.ds(c * ROWS, ROWS), :] = outs[2 * k + c]
                        else:
                            r1s[i, r, pl.ds(c * ROWS, ROWS), :] = outs[2 * k + c]
                    level = jnp.where(low_half, rows[2 * k], rows[2 * k + 1])
                    wanted = jnp.where(low_half, request[2 * k], request[2 * k + 1]) + half * NEW
                    filled = jnp.where(low_half, request[2 * k], request[2 * k + 1]) < NEW
                    tiles[r] = jnp.where((tile_row == wanted) & filled, level, tiles[r])
                    if r > 0 and half == halves[0]:
                        send_part(i, r)
        for r in range(PEERS):
            if r == 0:
                st[ip, 0] = tiles[0]
            else:
                sts[ip, r] = tiles[r]
                send_level(ip, r)
                send_part(2 * ip + halves[1], r)

    def partial_step(ip, carry):
        partial_pair(ip, True)
        return carry

    lax.fori_loop(1, NZ // 2, partial_step, 0)
    partial_pair(jnp.int32(0), True, (1, 0))

    for copy in mig_copies:
        copy.wait()
    bit = partner_bit[me]
    hand_here = migrate_out[me]
    hand_there = lax.select(bit == 0, migrate_out[partners[0]], migrate_out[partners[1]])
    nothing = jnp.zeros((ROWS, HD), jnp.bfloat16)
    for r in range(RES):
        attm[pl.ds(r * ROWS, ROWS), :] = lax.select(
            r < RES - hand_here, att[pl.ds(r * ROWS, ROWS), :], nothing
        )
    for m in range(MIG):
        came = lax.select(
            bit == 0, guest[0, pl.ds(m * ROWS, ROWS), :], guest[1, pl.ds(m * ROWS, ROWS), :]
        )
        attm[pl.ds((RES + m) * ROWS, ROWS), :] = lax.select(
            m >= MIG - hand_there, came, nothing
        )

    def by_head(values, slots):
        size = slots * ROWS
        row = iota((size, size), 0)
        col = iota((size, size), 1)
        goal = (
            lax.rem(lax.div(row, STEPS), slots) * ROWS
            + lax.div(row, STEPS * slots) * STEPS
            + lax.rem(row, STEPS)
        )
        moved = dot(jnp.where(col == goal, 1.0, 0.0).astype(jnp.bfloat16), values)
        return moved.astype(jnp.bfloat16)

    moved = by_head(attm[...], RES + MIG)
    lead = (RES + MIG) * STEPS
    for h in range(ROWS // STEPS):
        xres[:, pl.ds(h * HD, HD)] = moved[h * lead : (h + 1) * lead]
    loads[4].wait()
    width = out.shape[1]

    def project(rows_ref, sends, send_sem, recv, recv_sem, own):
        copies = []
        for o in (3, 2, 1, 0):
            peer = tp_peer(o)
            part = dot(rows_ref[...], wv[:, pl.ds(pl.multiple_of(peer * width, width), width)])
            if o == 0:
                own[...] = part
            else:
                sends[o] = part.astype(jnp.bfloat16)
                copy = remote(sends.at[o], recv.at[o], send_sem.at[o], recv_sem.at[o], me, peer)
                copy.start()
                copies.append(copy)
        return copies

    rs1_copies = project(xres, rs1s, rs1_send, rs1, rs1_recv, own1)

    low = iota((2 * NEW, HD), 1) < 2 * ROWS

    def pair_levels(ip):
        drain(st.at[ip, pl.ds(1, PEERS - 1)], st_recv.at[ip])
        return [
            jnp.where(low, st[ip, 2 * q], st[ip, 2 * q + 1]) for q in range(PEERS // 2)
        ]

    def softmax_over(levels):
        m = levels[0]
        for level in levels[1:]:
            m = jnp.maximum(m, level)
        m = jnp.maximum(m, pltpu.roll(m, 2 * ROWS, 1))
        m = jnp.maximum(m, pltpu.roll(m, ROWS, 1))
        shares = [jnp.exp(level - m) for level in levels]
        total = shares[0]
        for share in shares[1:]:
            total = total + share
        total = total + pltpu.roll(total, 2 * ROWS, 1)
        total = total + pltpu.roll(total, ROWS, 1)
        return [share / total for share in shares], m + jnp.log(total)

    def merge(ip, levels, halves):
        shares, together = softmax_over(levels)
        ls[ip] = together
        for half in halves:
            i = 2 * ip + half
            drain(r1.at[i, pl.ds(1, PEERS - 1)], r1_recv.at[i])
            blocks = []
            for n in range(NEW):
                k = half * NEW + n
                blocks.append(
                    jnp.concatenate(
                        [jnp.where(diag, share[k : k + 1], 0.0) for share in shares], axis=1
                    )
                )
            mix = jnp.concatenate(blocks, axis=0).astype(jnp.bfloat16)
            merged = dot(mix, r1[i].reshape(PEERS * 2 * ROWS, HD)).astype(jnp.bfloat16)
            for n in range(NEW):
                r2s[i, n] = merged[n * ROWS : (n + 1) * ROWS]
            zi = order(i)
            turned = i + 1 - 2 * lax.rem(i + 1, 2)
            back = turned - lax.div(turned, NZ)
            remote(
                r2s.at[i], fin.at[:, back], r2_send.at[i], r2_recv.at[back], line(zi)
            ).start()
            remote(ls.at[ip], lf.at[back], lf_send.at[i], lf_recv.at[back], line(zi)).start()

    def merge_step(ip, carry):
        merge(ip, pair_levels(ip), (0, 1))
        return carry

    lax.fori_loop(1, NZ // 2, merge_step, 0)
    near = pair_levels(0)
    merge(jnp.int32(0), near, (1,))

    drain(r1.at[0, pl.ds(1, PEERS - 1)], r1_recv.at[0])
    for i in range(1, NZ):
        drain(lf.at[i], lf_recv.at[i])
        drain(fin.at[:, i], r2_recv.at[i])
    from_odd = [False, False, True, False, True, False, True, True]
    levels = [level[:NEW] for level in near]
    for base in range(0, NZ, 4):
        level = jnp.full((NEW, HD), LOW, jnp.float32)
        for g in range(4):
            i = base + g
            rows = lf[i, pl.ds(NEW if from_odd[i] else 0, NEW), :]
            level = jnp.where(quarter == g, rows, level)
        levels.append(level)
    shares, _ = softmax_over(levels)
    tail = NEW * STEPS
    row = iota((tail, HD), 0)
    spread = []
    for share in shares:
        wide = jnp.zeros((tail, HD), jnp.float32)
        for n in range(NEW):
            wide = jnp.where(lax.div(row, STEPS) == n, share[n : n + 1], wide)
        spread.append(wide)
    column = lax.rem(iota((tail, HD), 1), ROWS) - lax.rem(row, STEPS)
    owner = lax.div(row, STEPS)

    def mixing(parts, n):
        rows = []
        for h in range(ROWS // STEPS):
            keep = column == h * STEPS
            if n is not None:
                keep = keep & (owner == n)
            rows.append(
                jnp.concatenate([jnp.where(keep, part, 0.0) for part in parts], axis=1)
            )
        return jnp.concatenate(rows, axis=0).astype(jnp.bfloat16)

    attended = dot(mixing(spread[: PEERS // 2], None), r1[0].reshape(PEERS * 2 * ROWS, HD))
    for n in range(NEW):
        attended = attended + dot(
            mixing(spread[PEERS // 2 :], n), fin[n].reshape(NZ * ROWS, HD)
        )
    attended = attended.astype(jnp.bfloat16)
    for h in range(ROWS // STEPS):
        xnew[:, pl.ds(h * HD, HD)] = attended[h * tail : (h + 1) * tail]
    rs2_copies = project(xnew, rs2s, rs2_send, rs2, rs2_recv, own2)

    for copy in rs1_copies:
        copy.wait()
    total = own1[...]
    for o in range(1, TP):
        total = total + rs1[o].astype(jnp.float32)
    out[pl.ds(0, lead), :] = total.astype(jnp.bfloat16)
    for copy in q1_copies:
        copy.wait_send()
    for i in range(NZ):
        drain(fw.at[i, pl.ds(1, PEERS - 1)], q2_send.at[i])
        drain(r1s.at[i, pl.ds(1, PEERS - 1)], r1_send.at[i])
        if i > 0:
            drain(r2s.at[i], r2_send.at[i])
            drain(ls.at[i // 2], lf_send.at[i])
    for ip in range(NZ // 2):
        drain(sts.at[ip, pl.ds(1, PEERS - 1)], st_send.at[ip])
    for copy in rs2_copies:
        copy.wait()
    total = own2[...]
    for o in range(1, TP):
        total = total + rs2[o].astype(jnp.float32)
    out[pl.ds(lead, tail), :] = total.astype(jnp.bfloat16)


def per_device(
    res_keys,
    res_values,
    pool_keys,
    pool_values,
    queries,
    new_keys,
    new_values,
    res_len,
    new_len,
    page_source,
    page_index,
    partner_bit,
    migrate_out,
    out_weight,
):
    bf, f32 = jnp.bfloat16, jnp.float32
    rows = (RES + MIG + NEW) * STEPS
    lead, tail = (RES + MIG) * STEPS, NEW * STEPS
    width = out_weight.shape[1] // TP
    vmem = pl.BlockSpec(memory_space=pltpu.VMEM)
    hbm = pl.BlockSpec(memory_space=pltpu.HBM)
    dma = pltpu.SemaphoreType.DMA
    depth = out_weight.shape[0]
    whole = [
        pltpu.SMEM(res_len.shape, jnp.int32),
        pltpu.SMEM(new_len.shape, jnp.int32),
        pltpu.SMEM(partner_bit.shape, jnp.int32),
        pltpu.SMEM(migrate_out.shape, jnp.int32),
        pltpu.VMEM(page_source.shape, jnp.int32),
        pltpu.VMEM(page_index.shape, jnp.int32),
        pltpu.VMEM((queries.shape[0] * ROWS, HD), bf),
        pltpu.VMEM((queries.shape[0] * STEPS, HD), bf),
        pltpu.VMEM((queries.shape[0] * STEPS, HD), bf),
    ]
    scratch = whole + [
        pltpu.VMEM((RES, res_keys.shape[2], HD), bf),
        pltpu.VMEM((RES, res_keys.shape[2], HD), bf),
        pltpu.VMEM((pool_keys.shape[0], PAGE, HD), bf),
        pltpu.VMEM((pool_keys.shape[0], PAGE, HD), bf),
        pltpu.VMEM(out_weight.shape, bf),
        pltpu.VMEM((page_source.shape[0], HD), jnp.int32),
        pltpu.SMEM((page_source.shape[0], HD), jnp.int32),
        pltpu.VMEM((NZ, NEW * ROWS, HD), bf),
        pltpu.VMEM((NZ, PEERS, 2 * ROWS, HD), bf),
        pltpu.VMEM((NZ, PEERS, 2 * ROWS, HD), bf),
        pltpu.VMEM((NZ, PEERS, 2 * ROWS, HD), bf),
        pltpu.VMEM((NZ, PEERS, 2 * ROWS, HD), bf),
        pltpu.VMEM((NZ // 2, PEERS, 2 * NEW, HD), f32),
        pltpu.VMEM((NZ // 2, PEERS, 2 * NEW, HD), f32),
        pltpu.VMEM((NZ, NEW, ROWS, HD), bf),
        pltpu.VMEM((NZ // 2, 2 * NEW, HD), f32),
        pltpu.VMEM((NEW, NZ, ROWS, HD), bf),
        pltpu.VMEM((NZ, 2 * NEW, HD), f32),
        pltpu.VMEM((RES * ROWS, HD), bf),
        pltpu.VMEM((2, MIG * ROWS, HD), bf),
        pltpu.VMEM(((RES + MIG) * ROWS, HD), bf),
        pltpu.VMEM((lead, depth), bf),
        pltpu.VMEM((tail, depth), bf),
        pltpu.VMEM((lead, width), f32),
        pltpu.VMEM((tail, width), f32),
        pltpu.VMEM((TP, lead, width), bf),
        pltpu.VMEM((TP, lead, width), bf),
        pltpu.VMEM((TP, tail, width), bf),
        pltpu.VMEM((TP, tail, width), bf),
        dma((15,)),
        dma((NZ,)),
        dma((NZ,)),
        dma((NZ,)),
        dma((NZ,)),
        dma((NZ,)),
        dma((NZ,)),
        dma((NZ // 2,)),
        dma((NZ // 2,)),
        dma((NZ,)),
        dma((NZ,)),
        dma((NZ,)),
        dma((NZ,)),
        dma((2,)),
        dma((2,)),
        dma((TP,)),
        dma((TP,)),
        dma((TP,)),
        dma((TP,)),
    ]
    return pl.pallas_call(
        kernel,
        out_shape=jax.ShapeDtypeStruct((rows, width), bf),
        in_specs=[hbm] * 14,
        out_specs=vmem,
        scratch_shapes=scratch,
        compiler_params=pltpu.CompilerParams(
            collective_id=0, has_side_effects=True, vmem_limit_bytes=48 * 2**20
        ),
        cost_estimate=pl.CostEstimate(
            flops=10**9, bytes_accessed=16 * 2**20, transcendentals=10**6
        ),
    )(
        *(
            pltpu.with_memory_space_constraint(operand, pltpu.HBM)
            for operand in (
                res_len,
                new_len,
                partner_bit,
                migrate_out,
                page_source,
                page_index,
                queries.reshape(-1, HD),
                new_keys.reshape(-1, HD),
                new_values.reshape(-1, HD),
                res_keys.reshape(RES, -1, HD),
                res_values.reshape(RES, -1, HD),
                pool_keys.reshape(-1, PAGE, HD),
                pool_values.reshape(-1, PAGE, HD),
                out_weight,
            )
        )
    )


def solution(mesh):
    heads = P("inst", "tp", None, None)
    in_specs = (heads,) * 7 + (P(),) * 6 + (P("tp", None),)
    return jax.shard_map(
        per_device, mesh=mesh, in_specs=in_specs, out_specs=P("inst", "tp"), check_vma=False
    )
```
